256 devices in a mesh: seq: 32 (over y, z_hi, core), head: 8 (over z_lo, x).
Axes of the slice: x: 4, y: 4, z: 8 (z_hi: 4, z_lo: 2; z = z_hi * 2 + z_lo), core: 2. Of those that a mesh axis runs over, the one named last changes fastest.
Arguments:
- q_img: bfloat16 [2, 6144, 3072], P(None, ('seq', 'head')), may hold values from -140 to 140
- k_img: bfloat16 [2, 6144, 3072], P(None, ('seq', 'head')), may hold values from -6 to 6
- v_img: bfloat16 [2, 6144, 3072], P(None, ('seq', 'head')), may hold values from -6 to 6
- k_txt: bfloat16 [2, 512, 3072], P(None, 'seq', 'head'), may hold values from -8 to 8
- v_txt: bfloat16 [2, 512, 3072], P(None, 'seq', 'head'), may hold values from -6 to 6
- replace_cols: int32 [8], replicated, may hold values from 0 to 511
- shared_flags: int32 [512], replicated, may hold values 0 or 1
Outputs:
- attended: bfloat16 [2, 6144, 3072], P(None, ('seq', 'head'))
The draws below stay inside these ranges and needn't reach their ends.
All inputs are finite; a program needn't handle non-finite values.
Results may differ from the reference program's by a relative error of at most 0.0095.
Values may be sent and summed in bfloat16 or wider, within the bound.
No kernel may reach another device: no remote copies, remote signals or barrier semaphores. Data moves between devices by JAX's collectives and lax.ppermute only.
A program may use at most 128 MiB of HBM per device.

```python
import math
import jax
import jax.numpy as jnp
from jax import lax

H = 24
HD = 128
TXT = 512
REPL = 8
IMG = 6144


def draw_k_img(key, part):
    own_key = jax.random.fold_in(key, 3)
    return jnp.clip(jax.random.normal(own_key, (2, IMG, H * HD), jnp.float32), -6.0, 6.0).astype(jnp.bfloat16)


def draw_q_img(key, part):
    own_key = jax.random.fold_in(key, 7)
    return jnp.clip(jax.random.normal(own_key, (2, IMG, H * HD), jnp.float32), -6.0, 6.0).astype(jnp.bfloat16)


def place_ends(drawn, rng, low, high):
    place = [jax.random.randint(jax.random.fold_in(rng, axis), (), 0, length) for axis, length in enumerate(drawn.shape)]
    main_axis = drawn.shape.index(max(drawn.shape))
    beside = place[:main_axis] + [(place[main_axis] + 1) % drawn.shape[main_axis]] + place[main_axis + 1:]
    return drawn.at[tuple(place)].set(low).at[tuple(beside)].set(high)


def level_of(key, shape, cuts, least, largest):
    gain = 1.0
    for axis_at, shards_of in cuts:
        heights = jax.random.uniform(jax.random.fold_in(jax.random.fold_in(key, 6), axis_at), (shards_of,), jnp.float32, least / len(cuts), largest / len(cuts))
        gain = gain * jnp.repeat(jnp.exp(heights), shape[axis_at] // shards_of).reshape((-1,) + (1,) * (len(shape) - 1 - axis_at))
    return gain


def scatter_about(key, dims, spread, most, cuts=(), held_as=jnp.bfloat16):
    values = jax.random.normal(key, dims, jnp.float32) * spread
    if len(cuts) > 0:
        values = level_of(key, dims, cuts, -0.22, 0.18) * values
    return jnp.clip(values, min=-most, max=most).astype(held_as)


def setup_inputs(seed: int = 0) -> dict:
    streams_of = jax.random.split(jax.random.key(seed), 8)
    q_img = draw_q_img(jax.random.fold_in(streams_of[7], 71), 0)
    k_img = draw_k_img(jax.random.fold_in(streams_of[7], 71), 0)
    v_img = scatter_about(streams_of[2], (2, IMG, H * HD), 1.0, 6.0, ((1, 256),))
    k_txt = scatter_about(streams_of[3], (2, TXT, H * HD), 1.5, 8.0, ((1, 32), (2, 8)))
    v_txt = scatter_about(streams_of[4], (2, TXT, H * HD), 1.0, 6.0, ((1, 32), (2, 8)))
    replace_cols = place_ends(jax.random.randint(streams_of[5], (REPL,), 0, TXT), jax.random.fold_in(streams_of[5], 1), 0, TXT - 1).astype(jnp.int32)
    shared_flags = place_ends((jax.random.randint(streams_of[6], (TXT,), 0, 4) < 1).astype(jnp.int32), jax.random.fold_in(streams_of[6], 1), 0, 1)
    return dict(q_img=q_img, k_img=k_img, v_img=v_img, k_txt=k_txt, v_txt=v_txt, replace_cols=replace_cols, shared_flags=shared_flags)


def to_half(values):
    return lax.optimization_barrier(values.astype(jnp.bfloat16)).astype(jnp.float32)

def reference(q_img, k_img, v_img, k_txt, v_txt, replace_cols, shared_flags):
    score_scale = 1.0 / math.sqrt(HD)
    columns = jnp.arange(TXT, dtype=jnp.int32)
    listed = jnp.any(replace_cols[:, None] == columns[None, :], axis=0)
    edit_mask = jnp.logical_or(listed, shared_flags == 1).astype(jnp.float32)
    keys_all = jnp.concatenate([k_img, k_txt], axis=1)
    keep_rows = jnp.stack([jnp.ones_like(edit_mask), 1.0 - edit_mask])

    def one_head(head_index):
        start_col = (head_index * HD).astype(jnp.int32)
        head_query_rows = lax.dynamic_slice_in_dim(q_img, start_col, HD, 2).astype(jnp.float32)
        head_key_rows = lax.dynamic_slice_in_dim(keys_all, start_col, HD, 2).astype(jnp.float32)
        head_image_values = lax.dynamic_slice_in_dim(v_img, start_col, HD, 2).astype(jnp.float32)
        head_text_values = lax.dynamic_slice_in_dim(v_txt, start_col, HD, 2).astype(jnp.float32)
        logit_scores = jnp.einsum('msj,mzj->msz', head_query_rows, head_key_rows) * score_scale
        row_top = lax.optimization_barrier(jnp.max(logit_scores, axis=-1, keepdims=True))
        weights = jnp.exp(logit_scores - row_top)
        totals = lax.optimization_barrier(jnp.sum(weights, axis=-1, keepdims=True))
        image_retained = to_half(weights[:, :, :IMG])
        text_weights = weights[:, :, IMG:]
        text_retained = to_half(text_weights * keep_rows[:, None, :])
        weighted_numerator = jnp.einsum('hoe,heu->hou', image_retained, head_image_values) + jnp.einsum('hoe,heu->hou', text_retained, head_text_values)
        result = weighted_numerator / totals
        source_probs = text_weights[0] / totals[0]
        borrowed = to_half(source_probs * edit_mask[None, :])
        result = result.at[1].add(jnp.einsum('qk,kd->qd', borrowed, head_text_values[1]))
        return result
    stacked = lax.map(one_head, jnp.arange(H, dtype=jnp.int32))
    return jnp.transpose(stacked, (1, 2, 0, 3)).reshape(2, IMG, H * HD).astype(jnp.bfloat16)
```

```python
import functools
import math

import jax
import jax.numpy as jnp
import numpy as np
from jax import lax
from jax.experimental import pallas as pl
from jax.experimental.pallas import tpu as pltpu
from jax.sharding import Mesh
from jax.sharding import PartitionSpec as P

H = 24
HD = 128
LOG2E = 1.4426950408889634
SCALE2 = LOG2E / math.sqrt(HD)
VMEM_LIMIT = 56 * 1024 * 1024

VM = pl.BlockSpec(memory_space=pltpu.VMEM)
SM = pl.BlockSpec(memory_space=pltpu.SMEM)


def params():
    return pltpu.CompilerParams(vmem_limit_bytes=VMEM_LIMIT)


def pack_kernel(groups, q_ref, k_ref, v_ref, out_ref):
    width = q_ref.shape[2] // groups
    for group in range(groups):
        for branch in range(2):
            for at, ref in enumerate((q_ref, k_ref, v_ref)):
                out_ref[2 * group + branch, :, at * width : (at + 1) * width] = ref[
                    branch, :, group * width : (group + 1) * width
                ]


def pack(q, k, v, groups):
    rows, width = q.shape[1], q.shape[2] // groups
    return pl.pallas_call(
        functools.partial(pack_kernel, groups),
        out_shape=jax.ShapeDtypeStruct((2 * groups, rows, 3 * width), q.dtype),
        in_specs=[VM] * 3,
        out_specs=VM,
        compiler_params=params(),
    )(q, k, v)


def unpack_kernel(groups, in_ref, out_ref):
    width = in_ref.shape[2]
    for group in range(groups):
        for branch in range(2):
            out_ref[branch, :, group * width : (group + 1) * width] = in_ref[2 * group + branch]


def unpack(x, groups):
    return pl.pallas_call(
        functools.partial(unpack_kernel, groups),
        out_shape=jax.ShapeDtypeStruct((2, x.shape[1], groups * x.shape[2]), x.dtype),
        in_specs=[VM],
        out_specs=VM,
        compiler_params=params(),
    )(x)


def nt(a, b):
    return lax.dot_general(a, b, (((1,), (1,)), ((), ())), preferred_element_type=jnp.float32)


def nn(a, b):
    return lax.dot_general(a, b, (((1,), (0,)), ((), ())), preferred_element_type=jnp.float32)


def image_part(q, kv_refs, head, heads):
    cols = slice(head * HD, (head + 1) * HD)
    vcols = slice((heads + head) * HD, (heads + head + 1) * HD)
    scores = [nt(q, kv[:, cols]) for kv in kv_refs]
    top = scores[0].max(axis=-1, keepdims=True)
    for s in scores[1:]:
        top = jnp.maximum(top, s.max(axis=-1, keepdims=True))
    shift = top * SCALE2
    total = None
    acc = None
    for s, kv in zip(scores, kv_refs):
        w = jnp.exp2(s * SCALE2 - shift)
        t = w.sum(axis=-1, keepdims=True)
        a = nn(w.astype(jnp.bfloat16), kv[:, vcols])
        total = t if total is None else total + t
        acc = a if acc is None else acc + a
    return shift, total, acc


def block_kernel(heads, chunk, q_ref, kv0, kv1, kv2, kv3, out_ref, lse_ref):
    kvs = (kv0, kv1, kv2, kv3)
    rows = q_ref.shape[0]
    for head in range(heads):
        cols = slice(head * HD, (head + 1) * HD)
        for r in range(0, rows, chunk):
            shift, total, acc = image_part(q_ref[r : r + chunk, cols], kvs, head, heads)
            out_ref[r : r + chunk, cols] = (acc / total).astype(jnp.bfloat16)
            lse = jnp.broadcast_to(shift + jnp.log2(total), (chunk, HD))
            lse_ref[8 * head : 8 * head + 8, r : r + chunk] = lse.T[0:8]


def block_attention(q, kvs, heads, chunk=128):
    rows = q.shape[0]
    return pl.pallas_call(
        functools.partial(block_kernel, heads, chunk),
        out_shape=(
            jax.ShapeDtypeStruct((rows, heads * HD), jnp.bfloat16),
            jax.ShapeDtypeStruct((8 * heads, rows), jnp.float32),
        ),
        in_specs=[VM] * 5,
        out_specs=(VM, VM),
        compiler_params=params(),
        cost_estimate=pl.CostEstimate(
            flops=4 * heads * rows * HD * 4 * kvs[0].shape[0],
            bytes_accessed=4 * kvs[0].size * 2 + q.size * 4,
            transcendentals=heads * rows * 4 * kvs[0].shape[0],
        ),
    )(q, *kvs)


def own_kernel(
    heads, chunk, branch_ref, cols_ref, q_ref, kv0, kv1, kv2, kv3, text_ref, flags_ref,
    acc_ref, stat_ref, borrow_ref, kt, vt, vb,
):
    kvs = (kv0, kv1, kv2, kv3)
    rows = q_ref.shape[0]
    parts, _, per, _ = text_ref.shape
    txt = parts * per
    branch = branch_ref[0]
    for i in range(parts):
        kt[i * per : (i + 1) * per] = text_ref[i, branch]
        vt[i * per : (i + 1) * per] = text_ref[i, 2 + branch]
        vb[i * per : (i + 1) * per] = text_ref[i, 3]
    columns = lax.broadcasted_iota(jnp.int32, (1, txt), 1)
    listed = flags_ref[...] == 1
    for i in range(cols_ref.shape[0]):
        listed = jnp.logical_or(listed, columns == cols_ref[i])
    mask = listed.astype(jnp.float32)
    keep = 1.0 - mask * branch.astype(jnp.float32)
    for head in range(heads):
        cols = slice(head * HD, (head + 1) * HD)
        for r in range(0, rows, chunk):
            q = q_ref[r : r + chunk, cols]
            shift, total, acc = image_part(q, kvs, head, heads)
            s = nt(q, kt[:, cols])
            txt_shift = s.max(axis=-1, keepdims=True) * SCALE2
            overall = jnp.maximum(shift, txt_shift)
            factor = jnp.exp2(shift - overall)
            w = jnp.exp2(s * SCALE2 - overall)
            total = total * factor + w.sum(axis=-1, keepdims=True)
            acc = acc * factor + nn((w * keep).astype(jnp.bfloat16), vt[:, cols])
            borrow = nn((w * mask).astype(jnp.bfloat16), vb[:, cols])
            acc_ref[r : r + chunk, cols] = acc / total
            borrow_ref[r : r + chunk, cols] = borrow / total
            stat = jnp.broadcast_to(overall + jnp.log2(total), (chunk, HD))
            stat_ref[r : r + chunk, cols] = stat


def own_attention(branch, replace_cols, q, kvs, text, flags, heads, chunk=128):
    rows = q.shape[0]
    txt = text.shape[0] * text.shape[2]
    wide = jax.ShapeDtypeStruct((rows, heads * HD), jnp.float32)
    return pl.pallas_call(
        functools.partial(own_kernel, heads, chunk),
        out_shape=(wide, wide, wide),
        in_specs=[SM, SM] + [VM] * 7,
        out_specs=(VM, VM, VM),
        scratch_shapes=[pltpu.VMEM((txt, heads * HD), jnp.bfloat16)] * 3,
        compiler_params=params(),
        cost_estimate=pl.CostEstimate(
            flops=4 * heads * rows * HD * (4 * kvs[0].shape[0] + 2 * txt),
            bytes_accessed=4 * kvs[0].size * 2 + q.size * 4,
            transcendentals=heads * rows * (4 * kvs[0].shape[0] + txt),
        ),
    )(branch, replace_cols, q, *kvs, text, flags)


def merge_kernel(heads, chunk, acc_ref, stat_ref, borrow_ref, p1, p2, p3, l1, l2, l3, out_ref, lent_ref):
    rows = acc_ref.shape[0]
    for head in range(heads):
        cols = slice(head * HD, (head + 1) * HD)
        for r in range(0, rows, chunk):
            here = slice(r, r + chunk)
            own = stat_ref[here, cols]
            others = [
                jnp.broadcast_to(l[8 * head : 8 * head + 1, here], (HD, chunk)).T for l in (l1, l2, l3)
            ]
            top = own
            for o in others:
                top = jnp.maximum(top, o)
            own_w = jnp.exp2(own - top)
            weights = [jnp.exp2(o - top) for o in others]
            inverse = 1.0 / (own_w + weights[0] + weights[1] + weights[2])
            result = acc_ref[here, cols] * own_w
            for p, w in zip((p1, p2, p3), weights):
                result += p[here, cols].astype(jnp.float32) * w
            out_ref[here, cols] = result * inverse
            lent_ref[here, cols] = (borrow_ref[here, cols] * (own_w * inverse)).astype(jnp.bfloat16)


def merge(own, parts, stats, heads, chunk=128):
    rows = own[0].shape[0]
    return pl.pallas_call(
        functools.partial(merge_kernel, heads, chunk),
        out_shape=(
            jax.ShapeDtypeStruct((rows, heads * HD), jnp.float32),
            jax.ShapeDtypeStruct((rows, heads * HD), jnp.bfloat16),
        ),
        in_specs=[VM] * 9,
        out_specs=(VM, VM),
        compiler_params=params(),
    )(*own, *parts, *stats)


def ring(n, step):
    return [(i, (i + step) % n) for i in range(n)]


def body(q_img, k_img, v_img, k_txt, v_txt, replace_cols, shared_flags):
    groups = lax.axis_size("z_lo") * lax.axis_size("x")
    n_y, n_z = lax.axis_size("y"), lax.axis_size("z_hi")
    heads = H // groups
    width = heads * HD
    text = lax.all_gather(jnp.concatenate([k_txt, v_txt], axis=0), ("y", "z_hi", "core"), axis=0, tiled=False)
    packed = pack(q_img, k_img, v_img, groups)
    held = lax.all_to_all(packed, ("z_lo", "x", "core"), split_axis=0, concat_axis=0, tiled=True)
    rows = held.shape[0] * held.shape[1]
    held = held.reshape(rows, 3 * width)
    q, kv = held[:, :width], held[:, width:]
    kvs = [kv] + [lax.ppermute(kv, "y", ring(n_y, s)) for s in range(1, n_y)]
    parts, stats = [], []
    for s in (2, 1, 3):
        far_q = lax.ppermute(q, "z_hi", ring(n_z, s))
        part, stat = block_attention(far_q, kvs, heads)
        parts.append(lax.ppermute(part, "z_hi", ring(n_z, n_z - s)))
        stats.append(lax.ppermute(stat, "z_hi", ring(n_z, n_z - s)))
    branch = lax.axis_index("core").astype(jnp.int32)
    own = own_attention(branch.reshape(1), replace_cols, q, kvs, text, shared_flags.reshape(1, -1), heads)
    result, lent = merge(own, parts, stats, heads)
    borrowed = lax.ppermute(lent, "core", [(0, 1)])
    result = (result + borrowed.astype(jnp.float32)).astype(jnp.bfloat16)
    result = result.reshape(2 * groups, rows // (2 * groups), width)
    back = lax.all_to_all(result, ("z_lo", "x", "core"), split_axis=0, concat_axis=0, tiled=True)
    return unpack(back, groups)


def solution(mesh):
    fine = Mesh(mesh.devices.reshape(4, 4, 2, 2, 4), ("y", "z_hi", "core", "z_lo", "x"))
    seq, head = ("y", "z_hi", "core"), ("z_lo", "x")
    tokens = P(None, seq + head, None)
    text = P(None, seq, head)
    return jax.shard_map(
        body,
        mesh=fine,
        in_specs=(tokens, tokens, tokens, text, text, P(), P()),
        out_specs=tokens,
        check_vma=False,
    )
```

```python
import functools
import math

import jax
import jax.numpy as jnp
from jax import lax
from jax.experimental import pallas as pl
from jax.experimental.pallas import tpu as pltpu
from jax.sharding import Mesh
from jax.sharding import PartitionSpec as P

H = 24
HD = 128
LOG2E = 1.4426950408889634
SCALE2 = LOG2E / math.sqrt(HD)
VMEM_LIMIT = 24 * 1024 * 1024

VM = pl.BlockSpec(memory_space=pltpu.VMEM)
SM = pl.BlockSpec(memory_space=pltpu.SMEM)


def params(limit=VMEM_LIMIT):
    return pltpu.CompilerParams(vmem_limit_bytes=limit)


def pack_kernel(groups, q_ref, k_ref, v_ref, out_ref):
    width = q_ref.shape[2] // groups
    for group in range(groups):
        for branch in range(2):
            for at, ref in enumerate((q_ref, k_ref, v_ref)):
                out_ref[2 * group + branch, :, at * width : (at + 1) * width] = ref[
                    branch, :, group * width : (group + 1) * width
                ]


def pack(q, k, v, groups):
    rows, width = q.shape[1], q.shape[2] // groups
    return pl.pallas_call(
        functools.partial(pack_kernel, groups),
        out_shape=jax.ShapeDtypeStruct((2 * groups, rows, 3 * width), q.dtype),
        in_specs=[VM] * 3,
        out_specs=VM,
        compiler_params=params(2 * VMEM_LIMIT),
    )(q, k, v)


def unpack_kernel(groups, in_ref, out_ref):
    width = in_ref.shape[2]
    for group in range(groups):
        for branch in range(2):
            out_ref[branch, :, group * width : (group + 1) * width] = in_ref[2 * group + branch]


def unpack(x, groups):
    return pl.pallas_call(
        functools.partial(unpack_kernel, groups),
        out_shape=jax.ShapeDtypeStruct((2, x.shape[1], groups * x.shape[2]), x.dtype),
        in_specs=[VM],
        out_specs=VM,
        compiler_params=params(),
    )(x)


def split_kernel(core_ref, held_ref, own_ref, other_ref, q_ref, kv_ref):
    rows, width = held_ref.shape[0], q_ref.shape[1]
    per = own_ref.shape[1]
    core = core_ref[0]
    q_ref[0:rows, :] = held_ref[:, 0:width]
    kv_ref[...] = held_ref[:, width : 3 * width]
    for i, source in enumerate((core, 2 + core)):
        for ref, c in ((own_ref, core), (other_ref, 1 - core)):
            here = pl.ds(pl.multiple_of(rows + 2 * per * i + c * per, per), per)
            q_ref[here, :] = ref[source]


def split(core, held, own, other):
    rows, width = held.shape[0], held.shape[1] // 3
    return pl.pallas_call(
        split_kernel,
        out_shape=(
            jax.ShapeDtypeStruct((rows + 4 * own.shape[1], width), held.dtype),
            jax.ShapeDtypeStruct((rows, 2 * width), held.dtype),
        ),
        in_specs=[SM] + [VM] * 3,
        out_specs=(VM, VM),
        compiler_params=params(),
    )(core, held, own, other)


def nt(a, b):
    return lax.dot_general(a, b, (((1,), (1,)), ((), ())), preferred_element_type=jnp.float32)


def nn(a, b):
    return lax.dot_general(a, b, (((1,), (0,)), ((), ())), preferred_element_type=jnp.float32)


def write_stats(stat_ref, at, logs):
    rows = logs[0].shape[0]
    wide = [jnp.broadcast_to(log, (rows, HD)).T[0:16] for log in logs]
    line = lax.broadcasted_iota(jnp.int32, (16, rows), 0)
    x = jnp.where(line < 4, wide[0], jnp.where(line < 8, wide[1], wide[2]))
    high = x.astype(jnp.bfloat16).astype(jnp.float32)
    mid = (x - high).astype(jnp.bfloat16).astype(jnp.float32)
    low = x - high - mid
    part = jnp.bitwise_and(line, 3)
    x = jnp.where(part == 0, high, jnp.where(part == 1, mid, low))
    stat_ref[at : at + 16, :] = x.astype(jnp.bfloat16)


def read_stat(stats, head):
    return stats[4 * head : 4 * head + 1] + stats[4 * head + 1 : 4 * head + 2] + stats[4 * head + 2 : 4 * head + 3]


def head_cols(head, offset=0):
    return slice((offset + head) * HD, (offset + head + 1) * HD)


def take_block(refs, rows):
    whole = refs[0][...] if len(refs) == 1 else jnp.concatenate([ref[...] for ref in refs], axis=0)
    return whole[0:rows], whole[rows:]


def block_kernel(heads, n_q, n_kv, n_text, *refs):
    refs = list(refs)
    q_refs, kvs = [refs.pop(0) for _ in range(n_q)], [refs.pop(0) for _ in range(n_kv)]
    text_refs = [[refs.pop(0) for _ in range(n)] for n in n_text]
    refs.pop(0)
    out_ref = refs.pop(0)
    rows = out_ref.shape[0] - 16
    q, _ = take_block(q_refs, rows)

    def front(head):
        scores = [nt(q[:, head_cols(head)], kv[:, head_cols(head)]) for kv in kvs]
        top = scores[0].max(axis=-1, keepdims=True)
        for s in scores[1:]:
            top = jnp.maximum(top, s.max(axis=-1, keepdims=True))
        return scores, top * SCALE2

    ahead = front(0)
    logs = []
    for head in range(heads):
        scores, shift = ahead
        if head + 1 < heads:
            ahead = front(head + 1)
        total = acc = 0.0
        for s, kv in zip(scores, kvs):
            w = jnp.exp2(s * SCALE2 - shift)
            total = total + w.sum(axis=-1, keepdims=True)
            acc = acc + nn(w.astype(jnp.bfloat16), kv[:, head_cols(head, heads)])
        out_ref[0:rows, head_cols(head)] = (acc / total).astype(jnp.bfloat16)
        logs.append(shift + jnp.log2(total))
    write_stats(out_ref, rows, logs)
    for i, parts in enumerate(text_refs):
        refs[-1][i] = take_block(parts, rows)[1]


def block_attention(q, kvs, rows, heads, after, text_from=()):
    keys = sum(kv.shape[0] for kv in kvs)
    out = [jax.ShapeDtypeStruct((rows + 16, heads * HD), jnp.bfloat16)]
    if text_from:
        extra = sum(x.shape[0] for x in text_from[0]) - rows
        out.append(jax.ShapeDtypeStruct((len(text_from), extra, heads * HD), jnp.bfloat16))
    args = [*q, *kvs, *(x for block in text_from for x in block), after]
    return pl.pallas_call(
        functools.partial(block_kernel, heads, len(q), len(kvs), tuple(len(block) for block in text_from)),
        out_shape=out,
        in_specs=[VM] * len(args),
        out_specs=[VM] * len(out),
        compiler_params=params(),
        cost_estimate=pl.CostEstimate(
            flops=4 * heads * rows * HD * keys,
            bytes_accessed=4 * keys * heads * HD,
            transcendentals=heads * rows * keys,
        ),
    )(*args)


def text_kernel(heads, place_ref, cols_ref, q_ref, text_ref, values_ref, flags_ref, out_ref, lent_ref, kt, vt, vb):
    rows = lent_ref.shape[0]
    n_y, n_z, extra, _ = text_ref.shape
    per, txt = extra // 2, kt.shape[0]
    z, core = place_ref[0], place_ref[1]
    for y in range(n_y):
        for sz in range(n_z):
            here = pl.ds(pl.multiple_of((y * n_z + lax.rem(z + n_z - sz, n_z)) * per, per), per)
            kt[here, :] = text_ref[y, sz, 0:per]
            vt[here, :] = text_ref[y, sz, per : 2 * per]
            vb[here, :] = values_ref[1, y, sz]
    columns = lax.broadcasted_iota(jnp.int32, (1, txt), 1)
    listed = flags_ref[...] == 1
    for i in range(cols_ref.shape[0]):
        listed = jnp.logical_or(listed, columns == cols_ref[i])
    mask = listed.astype(jnp.float32)
    keep = 1.0 - mask * core.astype(jnp.float32)
    logs = []
    for head in range(heads):
        cols = head_cols(head)
        s = nt(q_ref[0:rows, cols], kt[:, cols])
        shift = s.max(axis=-1, keepdims=True) * SCALE2
        w = jnp.exp2(s * SCALE2 - shift)
        total = w.sum(axis=-1, keepdims=True)
        acc = nn((w * keep).astype(jnp.bfloat16), vt[:, cols])
        borrow = nn((w * mask).astype(jnp.bfloat16), vb[:, cols])
        out_ref[0:rows, cols] = (acc / total).astype(jnp.bfloat16)
        lent_ref[:, cols] = (borrow / total).astype(jnp.bfloat16)
        logs.append(shift + jnp.log2(total))
    write_stats(out_ref, rows, logs)


def text_attention(place, replace_cols, q, text, values, flags, rows, heads):
    txt = text.shape[0] * text.shape[1] * text.shape[2] // 2
    return pl.pallas_call(
        functools.partial(text_kernel, heads),
        out_shape=(
            jax.ShapeDtypeStruct((rows + 16, heads * HD), jnp.bfloat16),
            jax.ShapeDtypeStruct((rows, heads * HD), jnp.bfloat16),
        ),
        in_specs=[SM, SM] + [VM] * 4,
        out_specs=(VM, VM),
        scratch_shapes=[pltpu.VMEM((txt, heads * HD), jnp.bfloat16)] * 3,
        compiler_params=params(),
        cost_estimate=pl.CostEstimate(
            flops=6 * heads * rows * HD * txt,
            bytes_accessed=6 * txt * heads * HD,
            transcendentals=heads * rows * txt,
        ),
    )(place, replace_cols, q, text, values, flags)


def merge_kernel(heads, p0, p1, p2, p3, pt, lent_in, out_ref, lent_ref):
    parts = (p0, p1, p2, p3, pt)
    rows = lent_in.shape[0]
    stats = [p[rows : rows + 16].astype(jnp.float32) for p in parts]
    for head in range(heads):
        cols = head_cols(head)
        logs = [read_stat(s, head) for s in stats]
        top = functools.reduce(jnp.maximum, logs)
        weights = [jnp.exp2(log - top) for log in logs]
        inverse = 1.0 / sum(weights)
        weights = [jnp.broadcast_to(w * inverse, (HD, rows)).T for w in weights]
        result = 0.0
        for p, w in zip(parts, weights):
            result = result + p[0:rows, cols].astype(jnp.float32) * w
        out_ref[:, cols] = result
        lent_ref[:, cols] = (lent_in[:, cols].astype(jnp.float32) * weights[-1]).astype(jnp.bfloat16)


def merge(parts, lent, heads):
    rows = lent.shape[0]
    return pl.pallas_call(
        functools.partial(merge_kernel, heads),
        out_shape=(
            jax.ShapeDtypeStruct((rows, heads * HD), jnp.float32),
            jax.ShapeDtypeStruct((rows, heads * HD), jnp.bfloat16),
        ),
        in_specs=[VM] * 6,
        out_specs=(VM, VM),
        compiler_params=params(),
    )(*parts, lent)


def ring(n, step):
    return [(i, (i + step) % n) for i in range(n)]


def gather_ring(x, axis, n):
    near = {s: lax.ppermute(x, axis, ring(n, s)) for s in (1, n - 1)}
    half = x.shape[0] // 2
    far = [
        lax.ppermute(near[1][:half], axis, ring(n, 1)),
        lax.ppermute(near[n - 1][half:], axis, ring(n, n - 1)),
    ]
    return {1: [near[1]], n // 2: far, n - 1: [near[n - 1]]}


def body(q_img, k_img, v_img, k_txt, v_txt, replace_cols, shared_flags):
    groups = lax.axis_size("z_lo") * lax.axis_size("x")
    n_y, n_z = lax.axis_size("y"), lax.axis_size("z_hi")
    heads = H // groups
    width = heads * HD
    axes = ("z_lo", "x", "core")
    own_text = jnp.concatenate([k_txt, v_txt], axis=0)
    other_text = lax.ppermute(own_text, "core", [(0, 1), (1, 0)])
    packed = pack(q_img, k_img, v_img, groups)
    held = lax.all_to_all(packed, axes, split_axis=0, concat_axis=0, tiled=True)
    rows = held.shape[0] * held.shape[1]
    place = jnp.stack([lax.axis_index(a) for a in ("z_hi", "core")]).astype(jnp.int32)
    q, kv = split(place[1:], held.reshape(rows, 3 * width), own_text, other_text)
    qs = {0: [q]} | gather_ring(q, "z_hi", n_z)
    kvs = [kv] + [piece for block in gather_ring(kv, "y", n_y).values() for piece in block]
    flags = shared_flags.reshape(1, -1)
    parts, before = [], flags
    for s in (1, 3, 2):
        before = block_attention(qs[s], kvs, rows, heads, before)[0]
        parts.append(lax.ppermute(before, "z_hi", ring(n_z, n_z - s)))
    own, text = block_attention(qs[0], kvs, rows, heads, before, [qs[i] for i in range(n_z)])
    text = lax.all_gather(text, "y")
    values = lax.all_gather(text[:, :, text.shape[2] // 2 :], "core")
    txt_part, lent = text_attention(place, replace_cols, q, text, values, flags, rows, heads)
    result, lent = merge([own] + parts + [txt_part], lent, heads)
    borrowed = lax.ppermute(lent, "core", [(0, 1)])
    result = (result + borrowed.astype(jnp.float32)).astype(jnp.bfloat16)
    result = result.reshape(2 * groups, rows // (2 * groups), width)
    back = lax.all_to_all(result, axes, split_axis=0, concat_axis=0, tiled=True)
    return unpack(back, groups)


def solution(mesh):
    fine = Mesh(mesh.devices.reshape(4, 4, 2, 2, 4), ("y", "z_hi", "core", "z_lo", "x"))
    seq, head = ("y", "z_hi", "core"), ("z_lo", "x")
    tokens = P(None, seq + head, None)
    text = P(None, seq, head)
    return jax.shard_map(
        body,
        mesh=fine,
        in_specs=(tokens, tokens, tokens, text, text, P(), P()),
        out_specs=tokens,
        check_vma=False,
    )
```

```python
import functools
import math

import jax
import jax.numpy as jnp
from jax import lax
from jax.experimental import pallas as pl
from jax.experimental.pallas import tpu as pltpu
from jax.sharding import Mesh
from jax.sharding import PartitionSpec as P

H = 24
HD = 128
LOG2E = 1.4426950408889634
SCALE2 = LOG2E / math.sqrt(HD)
VMEM_LIMIT = 24 * 1024 * 1024

VM = pl.BlockSpec(memory_space=pltpu.VMEM)
SM = pl.BlockSpec(memory_space=pltpu.SMEM)


def params(limit=VMEM_LIMIT):
    return pltpu.CompilerParams(vmem_limit_bytes=limit)


def pack_kernel(groups, q_ref, k_ref, v_ref, out_ref, sem):
    width = q_ref.shape[2] // groups
    copies = []
    for group in range(groups):
        for branch in range(2):
            for at, ref in enumerate((q_ref, k_ref, v_ref)):
                copy = pltpu.make_async_copy(
                    ref.at[branch, :, pl.ds(group * width, width)],
                    out_ref.at[2 * group + branch, :, pl.ds(at * width, width)],
                    sem.at[len(copies)],
                )
                copy.start()
                copies.append(copy)
    for copy in copies:
        copy.wait()


def pack(q, k, v, groups):
    rows, width = q.shape[1], q.shape[2] // groups
    return pl.pallas_call(
        functools.partial(pack_kernel, groups),
        out_shape=jax.ShapeDtypeStruct((2 * groups, rows, 3 * width), q.dtype),
        in_specs=[pl.BlockSpec(memory_space=pl.ANY)] * 3,
        out_specs=VM,
        scratch_shapes=[pltpu.SemaphoreType.DMA((6 * groups,))],
        compiler_params=params(58 * 1024 * 1024),
    )(q, k, v)


def unpack_kernel(groups, in_ref, out_ref):
    width = in_ref.shape[2]
    for group in range(groups):
        for branch in range(2):
            out_ref[branch, :, group * width : (group + 1) * width] = in_ref[2 * group + branch]


def unpack(x, groups):
    return pl.pallas_call(
        functools.partial(unpack_kernel, groups),
        out_shape=jax.ShapeDtypeStruct((2, x.shape[1], groups * x.shape[2]), x.dtype),
        in_specs=[VM],
        out_specs=VM,
        compiler_params=params(),
    )(x)


def split_kernel(core_ref, held_ref, own_ref, other_ref, q_ref, kv_ref):
    rows, width = held_ref.shape[0], q_ref.shape[1]
    per = own_ref.shape[1]
    core = core_ref[0]
    q_ref[0:rows, :] = held_ref[:, 0:width]
    kv_ref[...] = held_ref[:, width : 3 * width]
    for i, source in enumerate((core, 2 + core)):
        for ref, c in ((own_ref, core), (other_ref, 1 - core)):
            here = pl.ds(pl.multiple_of(rows + 2 * per * i + c * per, per), per)
            q_ref[here, :] = ref[source]


def split(core, held, own, other):
    rows, width = held.shape[0], held.shape[1] // 3
    return pl.pallas_call(
        split_kernel,
        out_shape=(
            jax.ShapeDtypeStruct((rows + 4 * own.shape[1], width), held.dtype),
            jax.ShapeDtypeStruct((rows, 2 * width), held.dtype),
        ),
        in_specs=[SM] + [VM] * 3,
        out_specs=(VM, VM),
        compiler_params=params(),
    )(core, held, own, other)


def nt(a, b):
    return lax.dot_general(a, b, (((1,), (1,)), ((), ())), preferred_element_type=jnp.float32)


def nn(a, b):
    return lax.dot_general(a, b, (((1,), (0,)), ((), ())), preferred_element_type=jnp.float32)


def write_stats(stat_ref, at, logs):
    rows = logs[0].shape[0]
    wide = [jnp.broadcast_to(log, (rows, HD)).T[0:16] for log in logs]
    line = lax.broadcasted_iota(jnp.int32, (16, rows), 0)
    x = jnp.where(line < 4, wide[0], jnp.where(line < 8, wide[1], wide[2]))
    high = x.astype(jnp.bfloat16).astype(jnp.float32)
    mid = (x - high).astype(jnp.bfloat16).astype(jnp.float32)
    low = x - high - mid
    part = jnp.bitwise_and(line, 3)
    x = jnp.where(part == 0, high, jnp.where(part == 1, mid, low))
    stat_ref[at : at + 16, :] = x.astype(jnp.bfloat16)


def read_stat(stats, head):
    return stats[4 * head : 4 * head + 1] + stats[4 * head + 1 : 4 * head + 2] + stats[4 * head + 2 : 4 * head + 3]


def head_cols(head, offset=0):
    return slice((offset + head) * HD, (offset + head + 1) * HD)


def take_block(refs, rows):
    whole = refs[0][...] if len(refs) == 1 else jnp.concatenate([ref[...] for ref in refs], axis=0)
    return whole[0:rows], whole[rows:]


def attend(heads, q, kvs, out_ref):
    rows = out_ref.shape[0] - 16

    def front(head):
        scores = [nt(q[:, head_cols(head)], kv[:, head_cols(head)]) for kv in kvs]
        top = scores[0].max(axis=-1, keepdims=True)
        for s in scores[1:]:
            top = jnp.maximum(top, s.max(axis=-1, keepdims=True))
        return scores, top * SCALE2

    ahead = front(0)
    logs = []
    for head in range(heads):
        scores, shift = ahead
        if head + 1 < heads:
            ahead = front(head + 1)
        total = acc = 0.0
        for s, kv in zip(scores, kvs):
            w = jnp.exp2(s * SCALE2 - shift)
            total = total + w.sum(axis=-1, keepdims=True)
            acc = acc + nn(w.astype(jnp.bfloat16), kv[:, head_cols(head, heads)])
        out_ref[0:rows, head_cols(head)] = (acc / total).astype(jnp.bfloat16)
        logs.append(shift + jnp.log2(total))
    write_stats(out_ref, rows, logs)


def block_kernel(heads, n_q, n_kv, n_text, n_after, *refs):
    refs = list(refs)
    blocks = [[refs.pop(0) for _ in range(n)] for n in n_q]
    kvs = [refs.pop(0) for _ in range(n_kv)]
    texts = [[refs.pop(0) for _ in range(n)] for n in n_text]
    for _ in range(n_after):
        refs.pop(0)
    for block in blocks:
        out_ref = refs.pop(0)
        attend(heads, take_block(block, out_ref.shape[0] - 16)[0], kvs, out_ref)
    for i, parts in enumerate(texts):
        refs[0][i] = take_block(parts, kvs[0].shape[0])[1]


def block_attention(blocks, kvs, rows, heads, after, text_from=()):
    keys = sum(kv.shape[0] for kv in kvs)
    out = [jax.ShapeDtypeStruct((rows + 16, heads * HD), jnp.bfloat16)] * len(blocks)
    if text_from:
        extra = sum(x.shape[0] for x in text_from[0]) - rows
        out.append(jax.ShapeDtypeStruct((len(text_from), extra, heads * HD), jnp.bfloat16))
    args = [x for block in blocks for x in block] + kvs + [x for block in text_from for x in block] + list(after)
    return pl.pallas_call(
        functools.partial(
            block_kernel, heads, [len(b) for b in blocks], len(kvs), [len(b) for b in text_from], len(after)
        ),
        out_shape=out,
        in_specs=[VM] * len(args),
        out_specs=[VM] * len(out),
        compiler_params=params(),
        cost_estimate=pl.CostEstimate(
            flops=4 * len(blocks) * heads * rows * HD * keys,
            bytes_accessed=4 * keys * heads * HD,
            transcendentals=len(blocks) * heads * rows * keys,
        ),
    )(*args)


def text_kernel(heads, place_ref, cols_ref, q_ref, text_ref, values_ref, flags_ref, out_ref, lent_ref, kt, vt, vb):
    rows = lent_ref.shape[0]
    n_y, n_z, extra, _ = text_ref.shape
    per, txt = extra // 2, kt.shape[0]
    z, core = place_ref[0], place_ref[1]
    for y in range(n_y):
        for sz in range(n_z):
            here = pl.ds(pl.multiple_of((y * n_z + lax.rem(z + n_z - sz, n_z)) * per, per), per)
            kt[here, :] = text_ref[y, sz, 0:per]
            vt[here, :] = text_ref[y, sz, per : 2 * per]
            vb[here, :] = values_ref[1, y, sz]
    columns = lax.broadcasted_iota(jnp.int32, (1, txt), 1)
    listed = flags_ref[...] == 1
    for i in range(cols_ref.shape[0]):
        listed = jnp.logical_or(listed, columns == cols_ref[i])
    mask = listed.astype(jnp.float32)
    keep = 1.0 - mask * core.astype(jnp.float32)
    logs = []
    for head in range(heads):
        cols = head_cols(head)
        s = nt(q_ref[0:rows, cols], kt[:, cols])
        shift = s.max(axis=-1, keepdims=True) * SCALE2
        w = jnp.exp2(s * SCALE2 - shift)
        total = w.sum(axis=-1, keepdims=True)
        acc = nn((w * keep).astype(jnp.bfloat16), vt[:, cols])
        borrow = nn((w * mask).astype(jnp.bfloat16), vb[:, cols])
        out_ref[0:rows, cols] = (acc / total).astype(jnp.bfloat16)
        lent_ref[:, cols] = (borrow / total).astype(jnp.bfloat16)
        logs.append(shift + jnp.log2(total))
    write_stats(out_ref, rows, logs)


def text_attention(place, replace_cols, q, text, values, flags, rows, heads):
    txt = text.shape[0] * text.shape[1] * text.shape[2] // 2
    return pl.pallas_call(
        functools.partial(text_kernel, heads),
        out_shape=(
            jax.ShapeDtypeStruct((rows + 16, heads * HD), jnp.bfloat16),
            jax.ShapeDtypeStruct((rows, heads * HD), jnp.bfloat16),
        ),
        in_specs=[SM, SM] + [VM] * 4,
        out_specs=(VM, VM),
        scratch_shapes=[pltpu.VMEM((txt, heads * HD), jnp.bfloat16)] * 3,
        compiler_params=params(),
        cost_estimate=pl.CostEstimate(
            flops=6 * heads * rows * HD * txt,
            bytes_accessed=6 * txt * heads * HD,
            transcendentals=heads * rows * txt,
        ),
    )(place, replace_cols, q, text, values, flags)


def merge_kernel(heads, p0, p1, p2, p3, pt, lent_in, out_ref, lent_ref):
    parts = (p0, p1, p2, p3, pt)
    rows = lent_in.shape[0]
    stats = [p[rows : rows + 16].astype(jnp.float32) for p in parts]
    for head in range(heads):
        cols = head_cols(head)
        logs = [read_stat(s, head) for s in stats]
        top = functools.reduce(jnp.maximum, logs)
        weights = [jnp.exp2(log - top) for log in logs]
        inverse = 1.0 / sum(weights)
        weights = [jnp.broadcast_to(w * inverse, (HD, rows)).T for w in weights]
        result = 0.0
        for p, w in zip(parts, weights):
            result = result + p[0:rows, cols].astype(jnp.float32) * w
        out_ref[:, cols] = result
        lent_ref[:, cols] = (lent_in[:, cols].astype(jnp.float32) * weights[-1]).astype(jnp.bfloat16)


def merge(parts, lent, heads):
    rows = lent.shape[0]
    return pl.pallas_call(
        functools.partial(merge_kernel, heads),
        out_shape=(
            jax.ShapeDtypeStruct((rows, heads * HD), jnp.float32),
            jax.ShapeDtypeStruct((rows, heads * HD), jnp.bfloat16),
        ),
        in_specs=[VM] * 6,
        out_specs=(VM, VM),
        compiler_params=params(),
    )(*parts, lent)


def ring(n, step):
    return [(i, (i + step) % n) for i in range(n)]


def gather_ring(x, axis, n):
    near = {s: lax.ppermute(x, axis, ring(n, s)) for s in (1, n - 1)}
    half = x.shape[0] // 2
    far = [
        lax.ppermute(near[1][:half], axis, ring(n, 1)),
        lax.ppermute(near[n - 1][half:], axis, ring(n, n - 1)),
    ]
    return {1: [near[1]], n // 2: far, n - 1: [near[n - 1]]}


def body(q_img, k_img, v_img, k_txt, v_txt, replace_cols, shared_flags):
    groups = lax.axis_size("z_lo") * lax.axis_size("x")
    n_y, n_z = lax.axis_size("y"), lax.axis_size("z_hi")
    heads = H // groups
    width = heads * HD
    axes = ("z_lo", "x", "core")
    own_text = jnp.concatenate([k_txt, v_txt], axis=0)
    other_text = lax.ppermute(own_text, "core", [(0, 1), (1, 0)])
    packed = pack(q_img, k_img, v_img, groups)
    held = lax.all_to_all(packed, axes, split_axis=0, concat_axis=0, tiled=True)
    rows = held.shape[0] * held.shape[1]
    place = jnp.stack([lax.axis_index(a) for a in ("z_hi", "core")]).astype(jnp.int32)
    q, kv = split(place[1:], held.reshape(rows, 3 * width), own_text, other_text)
    qs = {0: [q]} | gather_ring(q, "z_hi", n_z)
    kvs = [kv] + [piece for block in gather_ring(kv, "y", n_y).values() for piece in block]
    flags = shared_flags.reshape(1, -1)
    near = block_attention([qs[1], qs[3]], kvs, rows, heads, [])
    far, own, text = block_attention([qs[2], qs[0]], kvs, rows, heads, near, [qs[i] for i in range(n_z)])
    parts = [lax.ppermute(x, "z_hi", ring(n_z, n_z - s)) for s, x in ((1, near[0]), (3, near[1]), (2, far))]
    text = lax.all_gather(text, "y")
    values = lax.all_gather(text[:, :, text.shape[2] // 2 :], "core")
    txt_part, lent = text_attention(place, replace_cols, q, text, values, flags, rows, heads)
    result, lent = merge([own] + parts + [txt_part], lent, heads)
    borrowed = lax.ppermute(lent, "core", [(0, 1)])
    result = (result + borrowed.astype(jnp.float32)).astype(jnp.bfloat16)
    result = result.reshape(2 * groups, rows // (2 * groups), width)
    back = lax.all_to_all(result, axes, split_axis=0, concat_axis=0, tiled=True)
    return unpack(back, groups)


def solution(mesh):
    fine = Mesh(mesh.devices.reshape(4, 4, 2, 2, 4), ("y", "z_hi", "core", "z_lo", "x"))
    seq, head = ("y", "z_hi", "core"), ("z_lo", "x")
    tokens = P(None, seq + head, None)
    text = P(None, seq, head)
    return jax.shard_map(
        body,
        mesh=fine,
        in_specs=(tokens, tokens, tokens, text, text, P(), P()),
        out_specs=tokens,
        check_vma=False,
    )
```

```python
import functools
import math

import jax
import jax.numpy as jnp
from jax import lax
from jax.experimental import pallas as pl
from jax.experimental.pallas import tpu as pltpu
from jax.sharding import Mesh
from jax.sharding import PartitionSpec as P

H = 24
HD = 128
LOG2E = 1.4426950408889634
SCALE2 = LOG2E / math.sqrt(HD)
VMEM_LIMIT = 24 * 1024 * 1024

VM = pl.BlockSpec(memory_space=pltpu.VMEM)
SM = pl.BlockSpec(memory_space=pltpu.SMEM)


def params(limit=VMEM_LIMIT):
    return pltpu.CompilerParams(vmem_limit_bytes=limit)


def pack_kernel(groups, q_ref, k_ref, v_ref, out_ref, sem):
    width = q_ref.shape[2] // groups
    copies = []
    for group in range(groups):
        for branch in range(2):
            for at, ref in enumerate((q_ref, k_ref, v_ref)):
                copy = pltpu.make_async_copy(
                    ref.at[branch, :, pl.ds(group * width, width)],
                    out_ref.at[2 * group + branch, :, pl.ds(at * width, width)],
                    sem.at[len(copies)],
                )
                copy.start()
                copies.append(copy)
    for copy in copies:
        copy.wait()


def pack(q, k, v, groups):
    rows, width = q.shape[1], q.shape[2] // groups
    return pl.pallas_call(
        functools.partial(pack_kernel, groups),
        out_shape=jax.ShapeDtypeStruct((2 * groups, rows, 3 * width), q.dtype),
        in_specs=[pl.BlockSpec(memory_space=pl.ANY)] * 3,
        out_specs=VM,
        scratch_shapes=[pltpu.SemaphoreType.DMA((6 * groups,))],
        compiler_params=params(58 * 1024 * 1024),
    )(q, k, v)


def unpack_kernel(groups, in_ref, out_ref):
    width = in_ref.shape[2]
    for group in range(groups):
        for branch in range(2):
            out_ref[branch, :, group * width : (group + 1) * width] = in_ref[2 * group + branch]


def unpack(x, groups):
    return pl.pallas_call(
        functools.partial(unpack_kernel, groups),
        out_shape=jax.ShapeDtypeStruct((2, x.shape[1], groups * x.shape[2]), x.dtype),
        in_specs=[VM],
        out_specs=VM,
        compiler_params=params(),
    )(x)


def split_kernel(core_ref, held_ref, own_ref, other_ref, q_ref, k_ref, v_ref):
    rows, width = held_ref.shape[0], q_ref.shape[1]
    per = own_ref.shape[1]
    core = core_ref[0]
    q_ref[0:rows, :] = held_ref[:, 0:width]
    k_ref[...] = held_ref[:, width : 2 * width]
    v_ref[...] = held_ref[:, 2 * width : 3 * width]
    for i, source in enumerate((core, 2 + core)):
        for ref, c in ((own_ref, core), (other_ref, 1 - core)):
            here = pl.ds(pl.multiple_of(rows + 2 * per * i + c * per, per), per)
            q_ref[here, :] = ref[source]


def split(core, held, own, other):
    rows, width = held.shape[0], held.shape[1] // 3
    return pl.pallas_call(
        split_kernel,
        out_shape=(
            jax.ShapeDtypeStruct((rows + 4 * own.shape[1], width), held.dtype),
            jax.ShapeDtypeStruct((rows, width), held.dtype),
            jax.ShapeDtypeStruct((rows, width), held.dtype),
        ),
        in_specs=[SM] + [VM] * 3,
        out_specs=(VM, VM, VM),
        compiler_params=params(),
    )(core, held, own, other)


def nt(a, b):
    return lax.dot_general(a, b, (((1,), (1,)), ((), ())), preferred_element_type=jnp.float32)


def nn(a, b):
    return lax.dot_general(a, b, (((1,), (0,)), ((), ())), preferred_element_type=jnp.float32)


def write_stats(stat_ref, at, logs):
    rows = logs[0].shape[0]
    wide = [jnp.broadcast_to(log, (rows, HD)).T[0:16] for log in logs]
    line = lax.broadcasted_iota(jnp.int32, (16, rows), 0)
    x = jnp.where(line < 4, wide[0], jnp.where(line < 8, wide[1], wide[2]))
    high = x.astype(jnp.bfloat16).astype(jnp.float32)
    mid = (x - high).astype(jnp.bfloat16).astype(jnp.float32)
    low = x - high - mid
    part = jnp.bitwise_and(line, 3)
    x = jnp.where(part == 0, high, jnp.where(part == 1, mid, low))
    stat_ref[at : at + 16, :] = x.astype(jnp.bfloat16)


def read_stat(stats, head):
    return stats[4 * head : 4 * head + 1] + stats[4 * head + 1 : 4 * head + 2] + stats[4 * head + 2 : 4 * head + 3]


def head_cols(head, offset=0):
    return slice((offset + head) * HD, (offset + head + 1) * HD)


def take_block(refs, rows):
    whole = refs[0][...] if len(refs) == 1 else jnp.concatenate([ref[...] for ref in refs], axis=0)
    return whole[0:rows], whole[rows:]


def attend(heads, q, keys, values, out_ref):
    rows = out_ref.shape[0] - 16

    def front(head):
        scores = [nt(q[:, head_cols(head)], k[:, head_cols(head)]) for k in keys]
        top = scores[0].max(axis=-1, keepdims=True)
        for s in scores[1:]:
            top = jnp.maximum(top, s.max(axis=-1, keepdims=True))
        return scores, top * SCALE2

    ahead = front(0)
    logs = []
    for head in range(heads):
        scores, shift = ahead
        if head + 1 < heads:
            ahead = front(head + 1)
        total = acc = 0.0
        for s, v in zip(scores, values):
            w = jnp.exp2(s * SCALE2 - shift)
            total = total + w.sum(axis=-1, keepdims=True)
            acc = acc + nn(w.astype(jnp.bfloat16), v[:, head_cols(head)])
        out_ref[0:rows, head_cols(head)] = (acc / total).astype(jnp.bfloat16)
        logs.append(shift + jnp.log2(total))
    write_stats(out_ref, rows, logs)


def block_kernel(heads, n_q, n_keys, n_text, n_after, *refs):
    refs = list(refs)
    blocks = [[refs.pop(0) for _ in range(n)] for n in n_q]
    keys = [refs.pop(0) for _ in range(n_keys)]
    values = [refs.pop(0) for _ in range(n_keys)]
    texts = [[refs.pop(0) for _ in range(n)] for n in n_text]
    for _ in range(n_after):
        refs.pop(0)
    for block in blocks:
        out_ref = refs.pop(0)
        attend(heads, take_block(block, out_ref.shape[0] - 16)[0], keys, values, out_ref)
    for i, parts in enumerate(texts):
        refs[0][i] = take_block(parts, keys[0].shape[0])[1]


def block_attention(blocks, keys, values, rows, heads, after, text_from=()):
    n_keys = sum(k.shape[0] for k in keys)
    out = [jax.ShapeDtypeStruct((rows + 16, heads * HD), jnp.bfloat16)] * len(blocks)
    if text_from:
        extra = sum(x.shape[0] for x in text_from[0]) - rows
        out.append(jax.ShapeDtypeStruct((len(text_from), extra, heads * HD), jnp.bfloat16))
    args = [x for block in blocks for x in block] + keys + values + [x for block in text_from for x in block] + list(after)
    return pl.pallas_call(
        functools.partial(
            block_kernel, heads, [len(b) for b in blocks], len(keys), [len(b) for b in text_from], len(after)
        ),
        out_shape=out,
        in_specs=[VM] * len(args),
        out_specs=[VM] * len(out),
        compiler_params=params(),
        cost_estimate=pl.CostEstimate(
            flops=4 * len(blocks) * heads * rows * HD * n_keys,
            bytes_accessed=4 * n_keys * heads * HD,
            transcendentals=len(blocks) * heads * rows * n_keys,
        ),
    )(*args)


def text_kernel(heads, place_ref, cols_ref, q_ref, text_ref, values_ref, flags_ref, out_ref, lent_ref, kt, vt, vb):
    rows = lent_ref.shape[0]
    n_y, n_z, extra, _ = text_ref.shape
    per, txt = extra // 2, kt.shape[0]
    z, core = place_ref[0], place_ref[1]
    for y in range(n_y):
        for sz in range(n_z):
            here = pl.ds(pl.multiple_of((y * n_z + lax.rem(z + n_z - sz, n_z)) * per, per), per)
            kt[here, :] = text_ref[y, sz, 0:per]
            vt[here, :] = text_ref[y, sz, per : 2 * per]
            vb[here, :] = values_ref[1, y, sz]
    columns = lax.broadcasted_iota(jnp.int32, (1, txt), 1)
    listed = flags_ref[...] == 1
    for i in range(cols_ref.shape[0]):
        listed = jnp.logical_or(listed, columns == cols_ref[i])
    mask = listed.astype(jnp.float32)
    keep = 1.0 - mask * core.astype(jnp.float32)
    logs = []
    for head in range(heads):
        cols = head_cols(head)
        s = nt(q_ref[0:rows, cols], kt[:, cols])
        shift = s.max(axis=-1, keepdims=True) * SCALE2
        w = jnp.exp2(s * SCALE2 - shift)
        total = w.sum(axis=-1, keepdims=True)
        acc = nn((w * keep).astype(jnp.bfloat16), vt[:, cols])
        borrow = nn((w * mask).astype(jnp.bfloat16), vb[:, cols])
        out_ref[0:rows, cols] = (acc / total).astype(jnp.bfloat16)
        lent_ref[:, cols] = (borrow / total).astype(jnp.bfloat16)
        logs.append(shift + jnp.log2(total))
    write_stats(out_ref, rows, logs)


def text_attention(place, replace_cols, q, text, values, flags, rows, heads):
    txt = text.shape[0] * text.shape[1] * text.shape[2] // 2
    return pl.pallas_call(
        functools.partial(text_kernel, heads),
        out_shape=(
            jax.ShapeDtypeStruct((rows + 16, heads * HD), jnp.bfloat16),
            jax.ShapeDtypeStruct((rows, heads * HD), jnp.bfloat16),
        ),
        in_specs=[SM, SM] + [VM] * 4,
        out_specs=(VM, VM),
        scratch_shapes=[pltpu.VMEM((txt, heads * HD), jnp.bfloat16)] * 3,
        compiler_params=params(),
        cost_estimate=pl.CostEstimate(
            flops=6 * heads * rows * HD * txt,
            bytes_accessed=6 * txt * heads * HD,
            transcendentals=heads * rows * txt,
        ),
    )(place, replace_cols, q, text, values, flags)


def merge_kernel(heads, p0, p1, p2, p3, pt, lent_in, out_ref, lent_ref):
    parts = (p0, p1, p2, p3, pt)
    rows = lent_in.shape[0]
    stats = [p[rows : rows + 16].astype(jnp.float32) for p in parts]
    for head in range(heads):
        cols = head_cols(head)
        logs = [read_stat(s, head) for s in stats]
        top = functools.reduce(jnp.maximum, logs)
        weights = [jnp.exp2(log - top) for log in logs]
        inverse = 1.0 / sum(weights)
        weights = [jnp.broadcast_to(w * inverse, (HD, rows)).T for w in weights]
        result = 0.0
        for p, w in zip(parts, weights):
            result = result + p[0:rows, cols].astype(jnp.float32) * w
        out_ref[:, cols] = result
        lent_ref[:, cols] = (lent_in[:, cols].astype(jnp.float32) * weights[-1]).astype(jnp.bfloat16)


def merge(parts, lent, heads):
    rows = lent.shape[0]
    return pl.pallas_call(
        functools.partial(merge_kernel, heads),
        out_shape=(
            jax.ShapeDtypeStruct((rows, heads * HD), jnp.float32),
            jax.ShapeDtypeStruct((rows, heads * HD), jnp.bfloat16),
        ),
        in_specs=[VM] * 6,
        out_specs=(VM, VM),
        compiler_params=params(),
    )(*parts, lent)


def ring(n, step):
    return [(i, (i + step) % n) for i in range(n)]


def gather_ring(x, axis, n):
    near = {s: lax.ppermute(x, axis, ring(n, s)) for s in (1, n - 1)}
    half = x.shape[0] // 2
    far = [
        lax.ppermute(near[1][:half], axis, ring(n, 1)),
        lax.ppermute(near[n - 1][half:], axis, ring(n, n - 1)),
    ]
    return {1: [near[1]], n // 2: far, n - 1: [near[n - 1]]}


def body(q_img, k_img, v_img, k_txt, v_txt, replace_cols, shared_flags):
    groups = lax.axis_size("z_lo") * lax.axis_size("x")
    n_y, n_z = lax.axis_size("y"), lax.axis_size("z_hi")
    heads = H // groups
    width = heads * HD
    axes = ("z_lo", "x", "core")
    own_text = jnp.concatenate([k_txt, v_txt], axis=0)
    other_text = lax.ppermute(own_text, "core", [(0, 1), (1, 0)])
    packed = pack(q_img, k_img, v_img, groups)
    held = lax.all_to_all(packed, axes, split_axis=0, concat_axis=0, tiled=True)
    rows = held.shape[0] * held.shape[1]
    place = jnp.stack([lax.axis_index(a) for a in ("z_hi", "core")]).astype(jnp.int32)
    q, k, v = split(place[1:], held.reshape(rows, 3 * width), own_text, other_text)
    qs = {0: [q]} | gather_ring(q, "z_hi", n_z)
    up, down = ring(n_y, 1), ring(n_y, n_y - 1)
    keys = [k, lax.ppermute(k, "y", up), lax.ppermute(k, "y", down)]
    values = [v, lax.ppermute(v, "y", up), lax.ppermute(v, "y", down)]
    keys.append(lax.ppermute(keys[1], "y", up))
    values.append(lax.ppermute(values[2], "y", down))
    flags = shared_flags.reshape(1, -1)
    near = block_attention([qs[1], qs[3]], keys, values, rows, heads, [])
    far, own, text = block_attention([qs[2], qs[0]], keys, values, rows, heads, near, [qs[i] for i in range(n_z)])
    parts = [lax.ppermute(x, "z_hi", ring(n_z, n_z - s)) for s, x in ((1, near[0]), (3, near[1]), (2, far))]
    text = lax.all_gather(text, "y")
    values = lax.all_gather(text[:, :, text.shape[2] // 2 :], "core")
    txt_part, lent = text_attention(place, replace_cols, q, text, values, flags, rows, heads)
    result, lent = merge([own] + parts + [txt_part], lent, heads)
    borrowed = lax.ppermute(lent, "core", [(0, 1)])
    result = (result + borrowed.astype(jnp.float32)).astype(jnp.bfloat16)
    result = result.reshape(2 * groups, rows // (2 * groups), width)
    back = lax.all_to_all(result, axes, split_axis=0, concat_axis=0, tiled=True)
    return unpack(back, groups)


def solution(mesh):
    fine = Mesh(mesh.devices.reshape(4, 4, 2, 2, 4), ("y", "z_hi", "core", "z_lo", "x"))
    seq, head = ("y", "z_hi", "core"), ("z_lo", "x")
    tokens = P(None, seq + head, None)
    text = P(None, seq, head)
    return jax.shard_map(
        body,
        mesh=fine,
        in_specs=(tokens, tokens, tokens, text, text, P(), P()),
        out_specs=tokens,
        check_vma=False,
    )
```

```python
import functools
import math

import jax
import jax.numpy as jnp
from jax import lax
from jax.experimental import pallas as pl
from jax.experimental.pallas import tpu as pltpu
from jax.sharding import Mesh
from jax.sharding import PartitionSpec as P

H = 24
HD = 128
LOG2E = 1.4426950408889634
SCALE2 = LOG2E / math.sqrt(HD)
VMEM_LIMIT = 24 * 1024 * 1024
PACK_LIMIT = 58 * 1024 * 1024

VM = pl.BlockSpec(memory_space=pltpu.VMEM)
SM = pl.BlockSpec(memory_space=pltpu.SMEM)


def params(limit=VMEM_LIMIT):
    return pltpu.CompilerParams(vmem_limit_bytes=limit)


def pack_kernel(groups, q_ref, k_ref, v_ref, out_ref):
    width = q_ref.shape[2] // groups
    for group in range(groups):
        for branch in range(2):
            for at, ref in enumerate((q_ref, k_ref, v_ref)):
                out_ref[2 * group + branch, :, at * width : (at + 1) * width] = ref[
                    branch, :, group * width : (group + 1) * width
                ]


def pack(q, k, v, groups):
    rows, width = q.shape[1], q.shape[2] // groups
    return pl.pallas_call(
        functools.partial(pack_kernel, groups),
        out_shape=jax.ShapeDtypeStruct((2 * groups, rows, 3 * width), q.dtype),
        in_specs=[VM] * 3,
        out_specs=VM,
        compiler_params=params(PACK_LIMIT),
    )(q, k, v)


def unpack_kernel(groups, in_ref, out_ref):
    width = in_ref.shape[2]
    for group in range(groups):
        for branch in range(2):
            out_ref[branch, :, group * width : (group + 1) * width] = in_ref[2 * group + branch]


def unpack(x, groups):
    return pl.pallas_call(
        functools.partial(unpack_kernel, groups),
        out_shape=jax.ShapeDtypeStruct((2, x.shape[1], groups * x.shape[2]), x.dtype),
        in_specs=[VM],
        out_specs=VM,
        compiler_params=params(),
    )(x)


def split_kernel(core_ref, held_ref, own_ref, other_ref, q_ref, k_ref, v_ref):
    rows, width = held_ref.shape[0], q_ref.shape[1]
    per = own_ref.shape[1]
    core = core_ref[0]
    q_ref[0:rows, :] = held_ref[:, 0:width]
    k_ref[...] = held_ref[:, width : 2 * width]
    v_ref[...] = held_ref[:, 2 * width : 3 * width]
    for i, source in enumerate((core, 2 + core)):
        for ref, c in ((own_ref, core), (other_ref, 1 - core)):
            here = pl.ds(pl.multiple_of(rows + 2 * per * i + c * per, per), per)
            q_ref[here, :] = ref[source]


def split(core, held, own, other):
    rows, width = held.shape[0], held.shape[1] // 3
    return pl.pallas_call(
        split_kernel,
        out_shape=(
            jax.ShapeDtypeStruct((rows + 4 * own.shape[1], width), held.dtype),
            jax.ShapeDtypeStruct((rows, width), held.dtype),
            jax.ShapeDtypeStruct((rows, width), held.dtype),
        ),
        in_specs=[SM] + [VM] * 3,
        out_specs=(VM, VM, VM),
        compiler_params=params(),
    )(core, held, own, other)


def nt(a, b):
    return lax.dot_general(a, b, (((1,), (1,)), ((), ())), preferred_element_type=jnp.float32)


def nn(a, b):
    return lax.dot_general(a, b, (((1,), (0,)), ((), ())), preferred_element_type=jnp.float32)


def write_stats(stat_ref, at, logs):
    rows = logs[0].shape[0]
    wide = [jnp.broadcast_to(log, (rows, HD)).T[0:16] for log in logs]
    line = lax.broadcasted_iota(jnp.int32, (16, rows), 0)
    x = jnp.where(line < 4, wide[0], jnp.where(line < 8, wide[1], wide[2]))
    high = x.astype(jnp.bfloat16).astype(jnp.float32)
    mid = (x - high).astype(jnp.bfloat16).astype(jnp.float32)
    low = x - high - mid
    part = jnp.bitwise_and(line, 3)
    x = jnp.where(part == 0, high, jnp.where(part == 1, mid, low))
    stat_ref[at : at + 16, :] = x.astype(jnp.bfloat16)


def read_stat(stats, head):
    return stats[4 * head : 4 * head + 1] + stats[4 * head + 1 : 4 * head + 2] + stats[4 * head + 2 : 4 * head + 3]


def head_cols(head, offset=0):
    return slice((offset + head) * HD, (offset + head + 1) * HD)


def take_block(refs, rows):
    whole = refs[0][...] if len(refs) == 1 else jnp.concatenate([ref[...] for ref in refs], axis=0)
    return whole[0:rows], whole[rows:]


def attend(heads, qs, keys, values, outs):
    rows = keys[0].shape[0]

    def front(block, head):
        q = qs[block][:, head_cols(head)]
        scores = [nt(q, k[:, head_cols(head)]) for k in keys]
        top = scores[0].max(axis=-1, keepdims=True)
        for s in scores[1:]:
            top = jnp.maximum(top, s.max(axis=-1, keepdims=True))
        return scores, top * SCALE2

    items = [(block, head) for block in range(len(qs)) for head in range(heads)]
    ahead = front(*items[0])
    logs = []
    for n, (block, head) in enumerate(items):
        scores, shift = ahead
        if n + 1 < len(items):
            ahead = front(*items[n + 1])
        total = acc = 0.0
        for s, v in zip(scores, values):
            w = jnp.exp2(s * SCALE2 - shift)
            total = total + w.sum(axis=-1, keepdims=True)
            acc = acc + nn(w.astype(jnp.bfloat16), v[:, head_cols(head)])
        outs[block][0:rows, head_cols(head)] = (acc / total).astype(jnp.bfloat16)
        logs.append(shift + jnp.log2(total))
        if head + 1 == heads:
            write_stats(outs[block], rows, logs[-heads:])


def log_of(n):
    return n.bit_length() - 1


def write_mask(n_z, z, cols_ref, flags_ref, mask_ref):
    txt = flags_ref.shape[1]
    columns = lax.broadcasted_iota(jnp.int32, (1, txt), 1)
    listed = flags_ref[...] == 1
    for i in range(cols_ref.shape[0]):
        listed = jnp.logical_or(listed, columns == cols_ref[i])
    mask = jnp.broadcast_to(listed.astype(jnp.float32), (16, txt)).astype(jnp.bfloat16)
    per = txt // (n_z * n_z)
    place = lax.broadcasted_iota(jnp.int32, (txt, txt), 1)
    pair = lax.shift_right_logical(place, log_of(per))
    steps = jnp.bitwise_and(pair, n_z - 1)
    pair = pair - steps + jnp.bitwise_and(z + n_z - steps, n_z - 1)
    column = pair * per + jnp.bitwise_and(place, per - 1)
    chosen = lax.broadcasted_iota(jnp.int32, (txt, txt), 0) == column
    mask_ref[...] = nn(mask, chosen.astype(jnp.float32).astype(jnp.bfloat16))[0:1]


def block_kernel(heads, n_q, n_keys, n_text, n_after, with_mask, *refs):
    refs = list(refs)
    blocks = [[refs.pop(0) for _ in range(n)] for n in n_q]
    keys = [refs.pop(0) for _ in range(n_keys)]
    values = [refs.pop(0) for _ in range(n_keys)]
    texts = [[refs.pop(0) for _ in range(n)] for n in n_text]
    for _ in range(n_after):
        refs.pop(0)
    if with_mask:
        place_ref, cols_ref, flags_ref = [refs.pop(0) for _ in range(3)]
        write_mask(4, place_ref[0], cols_ref, flags_ref, refs[-1])
    rows = keys[0].shape[0]
    attend(heads, [take_block(block, rows)[0] for block in blocks], keys, values, refs[: len(blocks)])
    for i, parts in enumerate(texts):
        text = take_block(parts, rows)[1]
        half = text.shape[0] // 2
        refs[-1][0, i] = text[:half]
        refs[-1][1, i] = text[half:]


def block_attention(blocks, keys, values, rows, heads, after, text_from=(), mask_from=()):
    n_keys = sum(k.shape[0] for k in keys)
    out = [jax.ShapeDtypeStruct((rows + 16, heads * HD), jnp.bfloat16)] * len(blocks)
    if text_from:
        half = (sum(x.shape[0] for x in text_from[0]) - rows) // 2
        out.append(jax.ShapeDtypeStruct((2, len(text_from), half, heads * HD), jnp.bfloat16))
    if mask_from:
        out.append(jax.ShapeDtypeStruct(mask_from[2].shape, jnp.float32))
    args = [x for block in blocks for x in block] + keys + values + [x for block in text_from for x in block]
    args += list(after)
    return pl.pallas_call(
        functools.partial(
            block_kernel,
            heads,
            [len(b) for b in blocks],
            len(keys),
            [len(b) for b in text_from],
            len(after),
            bool(mask_from),
        ),
        out_shape=out,
        in_specs=[VM] * len(args) + [SM, SM, VM][: len(mask_from)],
        out_specs=[VM] * len(out),
        compiler_params=params(),
        cost_estimate=pl.CostEstimate(
            flops=4 * len(blocks) * heads * rows * HD * n_keys,
            bytes_accessed=4 * n_keys * heads * HD,
            transcendentals=len(blocks) * heads * rows * n_keys,
        ),
    )(*args, *mask_from)


def text_kernel(heads, core_ref, q_ref, text_ref, values_ref, mask_ref, out_ref, lent_ref):
    rows = lent_ref.shape[0]
    n_y = text_ref.shape[0]
    mask = mask_ref[...]
    keep = 1.0 - mask * core_ref[0].astype(jnp.float32)

    def joined(pieces):
        return jnp.concatenate([piece.reshape(-1, HD) for piece in pieces], axis=0)

    def front(head):
        cols = head_cols(head)
        s = nt(q_ref[0:rows, cols], joined([text_ref[y, 0, :, :, cols] for y in range(n_y)]))
        return s, s.max(axis=-1, keepdims=True) * SCALE2

    ahead = front(0)
    logs = []
    for head in range(heads):
        cols = head_cols(head)
        s, shift = ahead
        if head + 1 < heads:
            ahead = front(head + 1)
        w = jnp.exp2(s * SCALE2 - shift)
        total = w.sum(axis=-1, keepdims=True)
        acc = nn((w * keep).astype(jnp.bfloat16), joined([text_ref[y, 1, :, :, cols] for y in range(n_y)]))
        borrow = nn((w * mask).astype(jnp.bfloat16), joined([values_ref[1, y, :, :, cols] for y in range(n_y)]))
        out_ref[0:rows, cols] = (acc / total).astype(jnp.bfloat16)
        lent_ref[:, cols] = (borrow / total).astype(jnp.bfloat16)
        logs.append(shift + jnp.log2(total))
    write_stats(out_ref, rows, logs)


def text_attention(core, q, text, values, mask, rows, heads):
    txt = mask.shape[1]
    return pl.pallas_call(
        functools.partial(text_kernel, heads),
        out_shape=(
            jax.ShapeDtypeStruct((rows + 16, heads * HD), jnp.bfloat16),
            jax.ShapeDtypeStruct((rows, heads * HD), jnp.bfloat16),
        ),
        in_specs=[SM] + [VM] * 4,
        out_specs=(VM, VM),
        compiler_params=params(),
        cost_estimate=pl.CostEstimate(
            flops=6 * heads * rows * HD * txt,
            bytes_accessed=6 * txt * heads * HD,
            transcendentals=heads * rows * txt,
        ),
    )(core, q, text, values, mask)


def merge_kernel(heads, p0, p1, p2, p3, pt, lent_in, out_ref, lent_ref):
    parts = (p0, p1, p2, p3, pt)
    rows = lent_in.shape[0]
    stats = [p[rows : rows + 16].astype(jnp.float32) for p in parts]
    for head in range(heads):
        cols = head_cols(head)
        logs = [read_stat(s, head) for s in stats]
        top = functools.reduce(jnp.maximum, logs)
        weights = [jnp.exp2(log - top) for log in logs]
        inverse = 1.0 / sum(weights)
        weights = [jnp.broadcast_to(w * inverse, (HD, rows)).T for w in weights]
        result = 0.0
        for p, w in zip(parts, weights):
            result = result + p[0:rows, cols].astype(jnp.float32) * w
        out_ref[:, cols] = result
        lent_ref[:, cols] = (lent_in[:, cols].astype(jnp.float32) * weights[-1]).astype(jnp.bfloat16)


def merge(parts, lent, heads):
    rows = lent.shape[0]
    return pl.pallas_call(
        functools.partial(merge_kernel, heads),
        out_shape=(
            jax.ShapeDtypeStruct((rows, heads * HD), jnp.float32),
            jax.ShapeDtypeStruct((rows, heads * HD), jnp.bfloat16),
        ),
        in_specs=[VM] * 6,
        out_specs=(VM, VM),
        compiler_params=params(),
    )(*parts, lent)


def ring(n, step):
    return [(i, (i + step) % n) for i in range(n)]


def gather_ring(x, axis, n):
    near = {s: lax.ppermute(x, axis, ring(n, s)) for s in (1, n - 1)}
    half = x.shape[0] // 2
    far = [
        lax.ppermute(near[1][:half], axis, ring(n, 1)),
        lax.ppermute(near[n - 1][half:], axis, ring(n, n - 1)),
    ]
    return {1: [near[1]], n // 2: far, n - 1: [near[n - 1]]}


def body(q_img, k_img, v_img, k_txt, v_txt, replace_cols, shared_flags):
    groups = lax.axis_size("z_lo") * lax.axis_size("x")
    n_y, n_z = lax.axis_size("y"), lax.axis_size("z_hi")
    heads = H // groups
    width = heads * HD
    axes = ("z_lo", "x", "core")
    own_text = jnp.concatenate([k_txt, v_txt], axis=0)
    other_text = lax.ppermute(own_text, "core", [(0, 1), (1, 0)])
    packed = pack(q_img, k_img, v_img, groups)
    held = lax.all_to_all(packed, axes, split_axis=0, concat_axis=0, tiled=True)
    rows = held.shape[0] * held.shape[1]
    place = jnp.stack([lax.axis_index(a) for a in ("z_hi", "core")]).astype(jnp.int32)
    q, k, v = split(place[1:], held.reshape(rows, 3 * width), own_text, other_text)
    qs = {0: [q]} | gather_ring(q, "z_hi", n_z)
    up, down = ring(n_y, 1), ring(n_y, n_y - 1)
    keys = [k, lax.ppermute(k, "y", up), lax.ppermute(k, "y", down)]
    values = [v, lax.ppermute(v, "y", up), lax.ppermute(v, "y", down)]
    keys.append(lax.ppermute(keys[1], "y", up))
    values.append(lax.ppermute(values[2], "y", down))
    flags = shared_flags.reshape(1, -1)
    mask_from = (place[:1], replace_cols, flags)
    *near, mask = block_attention([qs[1], qs[3]], keys, values, rows, heads, [], mask_from=mask_from)
    far = block_attention([qs[2]], keys, values, rows, heads, near)
    own, text = block_attention([qs[0]], keys, values, rows, heads, far, [qs[i] for i in range(n_z)])
    far = far[0]
    parts = [lax.ppermute(x, "z_hi", ring(n_z, n_z - s)) for s, x in ((1, near[0]), (3, near[1]), (2, far))]
    text = lax.all_gather(text, "y")
    values = lax.all_gather(text[:, 1], "core")
    txt_part, lent = text_attention(place[1:], q, text, values, mask, rows, heads)
    result, lent = merge([own] + parts + [txt_part], lent, heads)
    borrowed = lax.ppermute(lent, "core", [(0, 1)])
    result = (result + borrowed.astype(jnp.float32)).astype(jnp.bfloat16)
    result = result.reshape(2 * groups, rows // (2 * groups), width)
    back = lax.all_to_all(result, axes, split_axis=0, concat_axis=0, tiled=True)
    return unpack(back, groups)


def solution(mesh):
    fine = Mesh(mesh.devices.reshape(4, 4, 2, 2, 4), ("y", "z_hi", "core", "z_lo", "x"))
    seq, head = ("y", "z_hi", "core"), ("z_lo", "x")
    tokens = P(None, seq + head, None)
    text = P(None, seq, head)
    return jax.shard_map(
        body,
        mesh=fine,
        in_specs=(tokens, tokens, tokens, text, text, P(), P()),
        out_specs=tokens,
        check_vma=False,
    )
```

```python
import functools
import math

import jax
import jax.numpy as jnp
from jax import lax
from jax.experimental import pallas as pl
from jax.experimental.pallas import tpu as pltpu
from jax.sharding import Mesh
from jax.sharding import PartitionSpec as P

H = 24
HD = 128
LOG2E = 1.4426950408889634
SCALE2 = LOG2E / math.sqrt(HD)
VMEM_LIMIT = 24 * 1024 * 1024
PACK_LIMIT = 58 * 1024 * 1024

VM = pl.BlockSpec(memory_space=pltpu.VMEM)
SM = pl.BlockSpec(memory_space=pltpu.SMEM)


def params(limit=VMEM_LIMIT):
    return pltpu.CompilerParams(vmem_limit_bytes=limit)


def pack_kernel(groups, q_ref, k_ref, v_ref, out_ref):
    width = q_ref.shape[2] // groups
    for group in range(groups):
        for branch in range(2):
            for at, ref in enumerate((q_ref, k_ref, v_ref)):
                out_ref[2 * group + branch, :, at * width : (at + 1) * width] = ref[
                    branch, :, group * width : (group + 1) * width
                ]


def pack(q, k, v, groups):
    rows, width = q.shape[1], q.shape[2] // groups
    return pl.pallas_call(
        functools.partial(pack_kernel, groups),
        out_shape=jax.ShapeDtypeStruct((2 * groups, rows, 3 * width), q.dtype),
        in_specs=[VM] * 3,
        out_specs=VM,
        compiler_params=params(PACK_LIMIT),
    )(q, k, v)


def unpack_kernel(groups, in_ref, out_ref):
    width = in_ref.shape[2]
    for group in range(groups):
        for branch in range(2):
            out_ref[branch, :, group * width : (group + 1) * width] = in_ref[2 * group + branch]


def unpack(x, groups):
    return pl.pallas_call(
        functools.partial(unpack_kernel, groups),
        out_shape=jax.ShapeDtypeStruct((2, x.shape[1], groups * x.shape[2]), x.dtype),
        in_specs=[VM],
        out_specs=VM,
        compiler_params=params(),
    )(x)


def split_kernel(core_ref, held_ref, own_ref, other_ref, q_ref, k_ref, v_ref):
    rows, width = held_ref.shape[0], q_ref.shape[1]
    per = own_ref.shape[1]
    core = core_ref[0]
    q_ref[0:rows, :] = held_ref[:, 0:width]
    k_ref[...] = held_ref[:, width : 2 * width]
    v_ref[...] = held_ref[:, 2 * width : 3 * width]
    for i, source in enumerate((core, 2 + core)):
        for ref, c in ((own_ref, core), (other_ref, 1 - core)):
            here = pl.ds(pl.multiple_of(rows + 2 * per * i + c * per, per), per)
            q_ref[here, :] = ref[source]


def split(core, held, own, other):
    rows, width = held.shape[0], held.shape[1] // 3
    return pl.pallas_call(
        split_kernel,
        out_shape=(
            jax.ShapeDtypeStruct((rows + 4 * own.shape[1], width), held.dtype),
            jax.ShapeDtypeStruct((rows, width), held.dtype),
            jax.ShapeDtypeStruct((rows, width), held.dtype),
        ),
        in_specs=[SM] + [VM] * 3,
        out_specs=(VM, VM, VM),
        compiler_params=params(),
    )(core, held, own, other)


def nt(a, b):
    return lax.dot_general(a, b, (((1,), (1,)), ((), ())), preferred_element_type=jnp.float32)


def nn(a, b):
    return lax.dot_general(a, b, (((1,), (0,)), ((), ())), preferred_element_type=jnp.float32)


def write_stats(stat_ref, at, logs):
    rows = logs[0].shape[0]
    wide = [jnp.broadcast_to(log, (rows, HD)).T[0:16] for log in logs]
    line = lax.broadcasted_iota(jnp.int32, (16, rows), 0)
    x = jnp.where(line < 4, wide[0], jnp.where(line < 8, wide[1], wide[2]))
    high = x.astype(jnp.bfloat16).astype(jnp.float32)
    mid = (x - high).astype(jnp.bfloat16).astype(jnp.float32)
    low = x - high - mid
    part = jnp.bitwise_and(line, 3)
    x = jnp.where(part == 0, high, jnp.where(part == 1, mid, low))
    stat_ref[at : at + 16, :] = x.astype(jnp.bfloat16)


def read_stat(stats, head):
    return stats[4 * head : 4 * head + 1] + stats[4 * head + 1 : 4 * head + 2] + stats[4 * head + 2 : 4 * head + 3]


def head_cols(head, offset=0):
    return slice((offset + head) * HD, (offset + head + 1) * HD)


def take_rows(refs, first, last, cols):
    pieces, at = [], 0
    for ref in refs:
        low, high = max(first - at, 0), min(last - at, ref.shape[0])
        if low < high:
            pieces.append(ref[low:high, cols])
        at += ref.shape[0]
    return pieces[0] if len(pieces) == 1 else jnp.concatenate(pieces, axis=0)


def attend(heads, qs, keys, values, outs):
    rows = keys[0].shape[0]

    def joined(refs, head):
        return jnp.concatenate([ref[:, head_cols(head)] for ref in refs], axis=0)

    def front(block, head):
        s = nt(take_rows(qs[block], 0, rows, head_cols(head)), joined(keys, head))
        return s, s.max(axis=-1, keepdims=True) * SCALE2

    items = [(block, head) for block in range(len(qs)) for head in range(heads)]
    ahead = front(*items[0])
    logs = []
    for n, (block, head) in enumerate(items):
        s, shift = ahead
        if n + 1 < len(items):
            ahead = front(*items[n + 1])
        w = jnp.exp2(s * SCALE2 - shift)
        total = w.sum(axis=-1, keepdims=True)
        acc = nn(w.astype(jnp.bfloat16), joined(values, head))
        outs[block][0:rows, head_cols(head)] = (acc / total).astype(jnp.bfloat16)
        logs.append(shift + jnp.log2(total))
        if head + 1 == heads:
            write_stats(outs[block], rows, logs[-heads:])


def log_of(n):
    return n.bit_length() - 1


def write_mask(n_z, z, cols_ref, flags_ref, mask_ref):
    txt = flags_ref.shape[1]
    columns = lax.broadcasted_iota(jnp.int32, (1, txt), 1)
    listed = flags_ref[...] == 1
    for i in range(cols_ref.shape[0]):
        listed = jnp.logical_or(listed, columns == cols_ref[i])
    mask = jnp.broadcast_to(listed.astype(jnp.float32), (16, txt)).astype(jnp.bfloat16)
    per = txt // (n_z * n_z)
    place = lax.broadcasted_iota(jnp.int32, (txt, txt), 1)
    pair = lax.shift_right_logical(place, log_of(per))
    steps = jnp.bitwise_and(pair, n_z - 1)
    pair = pair - steps + jnp.bitwise_and(z + n_z - steps, n_z - 1)
    column = pair * per + jnp.bitwise_and(place, per - 1)
    chosen = lax.broadcasted_iota(jnp.int32, (txt, txt), 0) == column
    mask_ref[...] = nn(mask, chosen.astype(jnp.float32).astype(jnp.bfloat16))[0:1]


def block_kernel(heads, n_q, n_keys, n_text, n_after, with_mask, *refs):
    refs = list(refs)
    blocks = [[refs.pop(0) for _ in range(n)] for n in n_q]
    keys = [refs.pop(0) for _ in range(n_keys)]
    values = [refs.pop(0) for _ in range(n_keys)]
    texts = [[refs.pop(0) for _ in range(n)] for n in n_text]
    for _ in range(n_after):
        refs.pop(0)
    if with_mask:
        place_ref, cols_ref, flags_ref = [refs.pop(0) for _ in range(3)]
        write_mask(4, place_ref[0], cols_ref, flags_ref, refs[-1])
    rows = keys[0].shape[0]
    attend(heads, blocks, keys, values, refs[: len(blocks)])
    for i, parts in enumerate(texts):
        half = refs[-1].shape[2]
        for kind in range(2):
            first = rows + kind * half
            refs[-1][kind, i] = take_rows(parts, first, first + half, slice(None))


def block_attention(blocks, keys, values, rows, heads, after, text_from=(), mask_from=()):
    n_keys = sum(k.shape[0] for k in keys)
    out = [jax.ShapeDtypeStruct((rows + 16, heads * HD), jnp.bfloat16)] * len(blocks)
    if text_from:
        half = (sum(x.shape[0] for x in text_from[0]) - rows) // 2
        out.append(jax.ShapeDtypeStruct((2, len(text_from), half, heads * HD), jnp.bfloat16))
    if mask_from:
        out.append(jax.ShapeDtypeStruct(mask_from[2].shape, jnp.float32))
    args = [x for block in blocks for x in block] + keys + values + [x for block in text_from for x in block]
    args += list(after)
    return pl.pallas_call(
        functools.partial(
            block_kernel,
            heads,
            [len(b) for b in blocks],
            len(keys),
            [len(b) for b in text_from],
            len(after),
            bool(mask_from),
        ),
        out_shape=out,
        in_specs=[VM] * len(args) + [SM, SM, VM][: len(mask_from)],
        out_specs=[VM] * len(out),
        compiler_params=params(),
        cost_estimate=pl.CostEstimate(
            flops=4 * len(blocks) * heads * rows * HD * n_keys,
            bytes_accessed=4 * n_keys * heads * HD,
            transcendentals=len(blocks) * heads * rows * n_keys,
        ),
    )(*args, *mask_from)


def text_kernel(heads, core_ref, q_ref, text_ref, values_ref, mask_ref, out_ref, lent_ref):
    rows = lent_ref.shape[0]
    n_y = text_ref.shape[0]
    mask = mask_ref[...]
    keep = 1.0 - mask * core_ref[0].astype(jnp.float32)

    def joined(pieces):
        return jnp.concatenate([piece.reshape(-1, HD) for piece in pieces], axis=0)

    def front(head):
        cols = head_cols(head)
        s = nt(q_ref[0:rows, cols], joined([text_ref[y, 0, :, :, cols] for y in range(n_y)]))
        return s, s.max(axis=-1, keepdims=True) * SCALE2

    ahead = front(0)
    logs = []
    for head in range(heads):
        cols = head_cols(head)
        s, shift = ahead
        if head + 1 < heads:
            ahead = front(head + 1)
        w = jnp.exp2(s * SCALE2 - shift)
        total = w.sum(axis=-1, keepdims=True)
        acc = nn((w * keep).astype(jnp.bfloat16), joined([text_ref[y, 1, :, :, cols] for y in range(n_y)]))
        borrow = nn((w * mask).astype(jnp.bfloat16), joined([values_ref[1, y, :, :, cols] for y in range(n_y)]))
        out_ref[0:rows, cols] = (acc / total).astype(jnp.bfloat16)
        lent_ref[:, cols] = (borrow / total).astype(jnp.bfloat16)
        logs.append(shift + jnp.log2(total))
    write_stats(out_ref, rows, logs)


def text_attention(core, q, text, values, mask, rows, heads):
    txt = mask.shape[1]
    return pl.pallas_call(
        functools.partial(text_kernel, heads),
        out_shape=(
            jax.ShapeDtypeStruct((rows + 16, heads * HD), jnp.bfloat16),
            jax.ShapeDtypeStruct((rows, heads * HD), jnp.bfloat16),
        ),
        in_specs=[SM] + [VM] * 4,
        out_specs=(VM, VM),
        compiler_params=params(),
        cost_estimate=pl.CostEstimate(
            flops=6 * heads * rows * HD * txt,
            bytes_accessed=6 * txt * heads * HD,
            transcendentals=heads * rows * txt,
        ),
    )(core, q, text, values, mask)


def merge_kernel(heads, p0, p1, p2, p3, pt, lent_in, out_ref, lent_ref):
    parts = (p0, p1, p2, p3, pt)
    rows = lent_in.shape[0]
    stats = [p[rows : rows + 16].astype(jnp.float32) for p in parts]
    for head in range(heads):
        cols = head_cols(head)
        logs = [read_stat(s, head) for s in stats]
        top = functools.reduce(jnp.maximum, logs)
        weights = [jnp.exp2(log - top) for log in logs]
        inverse = 1.0 / sum(weights)
        weights = [jnp.broadcast_to(w * inverse, (HD, rows)).T for w in weights]
        result = 0.0
        for p, w in zip(parts, weights):
            result = result + p[0:rows, cols].astype(jnp.float32) * w
        out_ref[:, cols] = result
        lent_ref[:, cols] = (lent_in[:, cols].astype(jnp.float32) * weights[-1]).astype(jnp.bfloat16)


def merge(parts, lent, heads):
    rows = lent.shape[0]
    return pl.pallas_call(
        functools.partial(merge_kernel, heads),
        out_shape=(
            jax.ShapeDtypeStruct((rows, heads * HD), jnp.float32),
            jax.ShapeDtypeStruct((rows, heads * HD), jnp.bfloat16),
        ),
        in_specs=[VM] * 6,
        out_specs=(VM, VM),
        compiler_params=params(),
    )(*parts, lent)


def ring(n, step):
    return [(i, (i + step) % n) for i in range(n)]


def gather_ring(x, axis, n):
    near = {s: lax.ppermute(x, axis, ring(n, s)) for s in (1, n - 1)}
    half = x.shape[0] // 2
    far = [
        lax.ppermute(near[1][:half], axis, ring(n, 1)),
        lax.ppermute(near[n - 1][half:], axis, ring(n, n - 1)),
    ]
    return {1: [near[1]], n // 2: far, n - 1: [near[n - 1]]}


def body(q_img, k_img, v_img, k_txt, v_txt, replace_cols, shared_flags):
    groups = lax.axis_size("z_lo") * lax.axis_size("x")
    n_y, n_z = lax.axis_size("y"), lax.axis_size("z_hi")
    heads = H // groups
    width = heads * HD
    axes = ("z_lo", "x", "core")
    own_text = jnp.concatenate([k_txt, v_txt], axis=0)
    other_text = lax.ppermute(own_text, "core", [(0, 1), (1, 0)])
    packed = pack(q_img, k_img, v_img, groups)
    held = lax.all_to_all(packed, axes, split_axis=0, concat_axis=0, tiled=True)
    rows = held.shape[0] * held.shape[1]
    place = jnp.stack([lax.axis_index(a) for a in ("z_hi", "core")]).astype(jnp.int32)
    q, k, v = split(place[1:], held.reshape(rows, 3 * width), own_text, other_text)
    qs = {0: [q]} | gather_ring(q, "z_hi", n_z)
    up, down = ring(n_y, 1), ring(n_y, n_y - 1)
    keys = [k, lax.ppermute(k, "y", up), lax.ppermute(k, "y", down)]
    values = [v, lax.ppermute(v, "y", up), lax.ppermute(v, "y", down)]
    keys.append(lax.ppermute(keys[1], "y", up))
    values.append(lax.ppermute(values[2], "y", down))
    flags = shared_flags.reshape(1, -1)
    mask_from = (place[:1], replace_cols, flags)
    *near, mask = block_attention([qs[1], qs[3]], keys, values, rows, heads, [], mask_from=mask_from)
    far = block_attention([qs[2]], keys, values, rows, heads, near)
    own, text = block_attention([qs[0]], keys, values, rows, heads, far, [qs[i] for i in range(n_z)])
    far = far[0]
    parts = [lax.ppermute(x, "z_hi", ring(n_z, n_z - s)) for s, x in ((1, near[0]), (3, near[1]), (2, far))]
    text = lax.all_gather(text, "y")
    values = lax.all_gather(text[:, 1], "core")
    txt_part, lent = text_attention(place[1:], q, text, values, mask, rows, heads)
    result, lent = merge([own] + parts + [txt_part], lent, heads)
    borrowed = lax.ppermute(lent, "core", [(0, 1)])
    result = (result + borrowed.astype(jnp.float32)).astype(jnp.bfloat16)
    result = result.reshape(2 * groups, rows // (2 * groups), width)
    back = lax.all_to_all(result, axes, split_axis=0, concat_axis=0, tiled=True)
    return unpack(back, groups)


def solution(mesh):
    fine = Mesh(mesh.devices.reshape(4, 4, 2, 2, 4), ("y", "z_hi", "core", "z_lo", "x"))
    seq, head = ("y", "z_hi", "core"), ("z_lo", "x")
    tokens = P(None, seq + head, None)
    text = P(None, seq, head)
    return jax.shard_map(
        body,
        mesh=fine,
        in_specs=(tokens, tokens, tokens, text, text, P(), P()),
        out_specs=tokens,
        check_vma=False,
    )
```

```python
import functools
import math

import jax
import jax.numpy as jnp
from jax import lax
from jax.experimental import pallas as pl
from jax.experimental.pallas import tpu as pltpu
from jax.sharding import Mesh
from jax.sharding import PartitionSpec as P

H = 24
HD = 128
LOG2E = 1.4426950408889634
SCALE2 = LOG2E / math.sqrt(HD)
VMEM_LIMIT = 24 * 1024 * 1024
PACK_LIMIT = 58 * 1024 * 1024

VM = pl.BlockSpec(memory_space=pltpu.VMEM)
SM = pl.BlockSpec(memory_space=pltpu.SMEM)


def params(limit=VMEM_LIMIT):
    return pltpu.CompilerParams(vmem_limit_bytes=limit)


def pack_kernel(groups, q_ref, k_ref, v_ref, out_ref):
    width = q_ref.shape[2] // groups
    for group in range(groups):
        for branch in range(2):
            for at, ref in enumerate((q_ref, k_ref, v_ref)):
                out_ref[2 * group + branch, :, at * width : (at + 1) * width] = ref[
                    branch, :, group * width : (group + 1) * width
                ]


def pack(q, k, v, groups):
    rows, width = q.shape[1], q.shape[2] // groups
    return pl.pallas_call(
        functools.partial(pack_kernel, groups),
        out_shape=jax.ShapeDtypeStruct((2 * groups, rows, 3 * width), q.dtype),
        in_specs=[VM] * 3,
        out_specs=VM,
        compiler_params=params(PACK_LIMIT),
    )(q, k, v)


def unpack_kernel(groups, in_ref, out_ref):
    width = in_ref.shape[2]
    for group in range(groups):
        for branch in range(2):
            out_ref[branch, :, group * width : (group + 1) * width] = in_ref[2 * group + branch]


def unpack(x, groups):
    return pl.pallas_call(
        functools.partial(unpack_kernel, groups),
        out_shape=jax.ShapeDtypeStruct((2, x.shape[1], groups * x.shape[2]), x.dtype),
        in_specs=[VM],
        out_specs=VM,
        compiler_params=params(),
    )(x)


def split_kernel(core_ref, held_ref, own_ref, other_ref, q_ref, k_ref, v_ref):
    rows, width = held_ref.shape[0], q_ref.shape[1]
    per = own_ref.shape[1]
    core = core_ref[0]
    q_ref[0:rows, :] = held_ref[:, 0:width]
    k_ref[...] = held_ref[:, width : 2 * width]
    v_ref[...] = held_ref[:, 2 * width : 3 * width]
    for i, source in enumerate((core, 2 + core)):
        for ref, c in ((own_ref, core), (other_ref, 1 - core)):
            here = pl.ds(pl.multiple_of(rows + 2 * per * i + c * per, per), per)
            q_ref[here, :] = ref[source]


def split(core, held, own, other):
    rows, width = held.shape[0], held.shape[1] // 3
    return pl.pallas_call(
        split_kernel,
        out_shape=(
            jax.ShapeDtypeStruct((rows + 4 * own.shape[1], width), held.dtype),
            jax.ShapeDtypeStruct((rows, width), held.dtype),
            jax.ShapeDtypeStruct((rows, width), held.dtype),
        ),
        in_specs=[SM] + [VM] * 3,
        out_specs=(VM, VM, VM),
        compiler_params=params(),
    )(core, held, own, other)


def nt(a, b):
    return lax.dot_general(a, b, (((1,), (1,)), ((), ())), preferred_element_type=jnp.float32)


def nn(a, b):
    return lax.dot_general(a, b, (((1,), (0,)), ((), ())), preferred_element_type=jnp.float32)


def write_stats(stat_ref, at, logs):
    rows = logs[0].shape[0]
    wide = [jnp.broadcast_to(log, (rows, HD)).T[0:16] for log in logs]
    line = lax.broadcasted_iota(jnp.int32, (16, rows), 0)
    x = jnp.where(line < 4, wide[0], jnp.where(line < 8, wide[1], wide[2]))
    high = x.astype(jnp.bfloat16).astype(jnp.float32)
    mid = (x - high).astype(jnp.bfloat16).astype(jnp.float32)
    low = x - high - mid
    part = jnp.bitwise_and(line, 3)
    x = jnp.where(part == 0, high, jnp.where(part == 1, mid, low))
    stat_ref[at : at + 16, :] = x.astype(jnp.bfloat16)


def read_stat(stats, head):
    return stats[4 * head : 4 * head + 1] + stats[4 * head + 1 : 4 * head + 2] + stats[4 * head + 2 : 4 * head + 3]


def head_cols(head, offset=0):
    return slice((offset + head) * HD, (offset + head + 1) * HD)


def take_rows(refs, first, last, cols):
    pieces, at = [], 0
    for ref in refs:
        low, high = max(first - at, 0), min(last - at, ref.shape[0])
        if low < high:
            pieces.append(ref[low:high, cols])
        at += ref.shape[0]
    return pieces[0] if len(pieces) == 1 else jnp.concatenate(pieces, axis=0)


def attend(heads, qs, keys, values, outs):
    rows = keys[0].shape[0]

    def joined(refs, head):
        return jnp.concatenate([ref[:, head_cols(head)] for ref in refs], axis=0)

    def front(block, head):
        s = nt(take_rows(qs[block], 0, rows, head_cols(head)), joined(keys, head))
        return s, s.max(axis=-1, keepdims=True) * SCALE2

    items = [(block, head) for block in range(len(qs)) for head in range(heads)]
    ahead = front(*items[0])
    logs = []
    for n, (block, head) in enumerate(items):
        s, shift = ahead
        if n + 1 < len(items):
            ahead = front(*items[n + 1])
        w = jnp.exp2(s * SCALE2 - shift)
        total = w.sum(axis=-1, keepdims=True)
        acc = nn(w.astype(jnp.bfloat16), joined(values, head))
        outs[block][0:rows, head_cols(head)] = (acc / total).astype(jnp.bfloat16)
        logs.append(shift + jnp.log2(total))
        if head + 1 == heads:
            write_stats(outs[block], rows, logs[-heads:])


def log_of(n):
    return n.bit_length() - 1


def write_mask(n_z, z, cols_ref, flags_ref, mask_ref):
    txt = flags_ref.shape[1]
    columns = lax.broadcasted_iota(jnp.int32, (1, txt), 1)
    listed = flags_ref[...] == 1
    for i in range(cols_ref.shape[0]):
        listed = jnp.logical_or(listed, columns == cols_ref[i])
    mask = jnp.broadcast_to(listed.astype(jnp.float32), (16, txt)).astype(jnp.bfloat16)
    per = txt // (n_z * n_z)
    place = lax.broadcasted_iota(jnp.int32, (txt, txt), 1)
    pair = lax.shift_right_logical(place, log_of(per))
    steps = jnp.bitwise_and(pair, n_z - 1)
    pair = pair - steps + jnp.bitwise_and(z + n_z - steps, n_z - 1)
    column = pair * per + jnp.bitwise_and(place, per - 1)
    chosen = lax.broadcasted_iota(jnp.int32, (txt, txt), 0) == column
    mask_ref[...] = nn(mask, chosen.astype(jnp.float32).astype(jnp.bfloat16))[0:1]


def block_kernel(heads, n_q, n_keys, n_text, n_after, with_mask, *refs):
    refs = list(refs)
    blocks = [[refs.pop(0) for _ in range(n)] for n in n_q]
    keys = [refs.pop(0) for _ in range(n_keys)]
    values = [refs.pop(0) for _ in range(n_keys)]
    texts = [[refs.pop(0) for _ in range(n)] for n in n_text]
    for _ in range(n_after):
        refs.pop(0)
    if with_mask:
        place_ref, cols_ref, flags_ref = [refs.pop(0) for _ in range(3)]
        write_mask(4, place_ref[0], cols_ref, flags_ref, refs[-1])
    rows = keys[0].shape[0]
    attend(heads, blocks, keys, values, refs[: len(blocks)])
    for i, parts in enumerate(texts):
        half = refs[-1].shape[2]
        for kind in range(2):
            first = rows + kind * half
            refs[-1][kind, i] = take_rows(parts, first, first + half, slice(None))


def block_attention(blocks, keys, values, rows, heads, after, text_from=(), mask_from=()):
    n_keys = sum(k.shape[0] for k in keys)
    out = [jax.ShapeDtypeStruct((rows + 16, heads * HD), jnp.bfloat16)] * len(blocks)
    if text_from:
        half = (sum(x.shape[0] for x in text_from[0]) - rows) // 2
        out.append(jax.ShapeDtypeStruct((2, len(text_from), half, heads * HD), jnp.bfloat16))
    if mask_from:
        out.append(jax.ShapeDtypeStruct(mask_from[2].shape, jnp.float32))
    args = [x for block in blocks for x in block] + keys + values + [x for block in text_from for x in block]
    args += list(after)
    return pl.pallas_call(
        functools.partial(
            block_kernel,
            heads,
            [len(b) for b in blocks],
            len(keys),
            [len(b) for b in text_from],
            len(after),
            bool(mask_from),
        ),
        out_shape=out,
        in_specs=[VM] * len(args) + [SM, SM, VM][: len(mask_from)],
        out_specs=[VM] * len(out),
        compiler_params=params(),
        cost_estimate=pl.CostEstimate(
            flops=4 * len(blocks) * heads * rows * HD * n_keys,
            bytes_accessed=4 * n_keys * heads * HD,
            transcendentals=len(blocks) * heads * rows * n_keys,
        ),
    )(*args, *mask_from)


def text_kernel(heads, core_ref, q_ref, text_ref, values_ref, mask_ref, out_ref, lent_ref):
    rows = lent_ref.shape[0]
    n_y = text_ref.shape[0]
    mask = mask_ref[...]
    keep = 1.0 - mask * core_ref[0].astype(jnp.float32)

    def joined(pieces):
        return jnp.concatenate([piece.reshape(-1, HD) for piece in pieces], axis=0)

    def front(head):
        cols = head_cols(head)
        s = nt(q_ref[0:rows, cols], joined([text_ref[y, 0, :, :, cols] for y in range(n_y)]))
        return s, s.max(axis=-1, keepdims=True) * SCALE2

    ahead = front(0)
    logs = []
    for head in range(heads):
        cols = head_cols(head)
        s, shift = ahead
        if head + 1 < heads:
            ahead = front(head + 1)
        w = jnp.exp2(s * SCALE2 - shift)
        total = w.sum(axis=-1, keepdims=True)
        acc = nn((w * keep).astype(jnp.bfloat16), joined([text_ref[y, 1, :, :, cols] for y in range(n_y)]))
        borrow = nn((w * mask).astype(jnp.bfloat16), joined([values_ref[1, y, :, :, cols] for y in range(n_y)]))
        out_ref[0:rows, cols] = (acc / total).astype(jnp.bfloat16)
        lent_ref[:, cols] = (borrow / total).astype(jnp.bfloat16)
        logs.append(shift + jnp.log2(total))
    write_stats(out_ref, rows, logs)


def text_attention(core, q, text, values, mask, rows, heads):
    txt = mask.shape[1]
    return pl.pallas_call(
        functools.partial(text_kernel, heads),
        out_shape=(
            jax.ShapeDtypeStruct((rows + 16, heads * HD), jnp.bfloat16),
            jax.ShapeDtypeStruct((rows, heads * HD), jnp.bfloat16),
        ),
        in_specs=[SM] + [VM] * 4,
        out_specs=(VM, VM),
        compiler_params=params(),
        cost_estimate=pl.CostEstimate(
            flops=6 * heads * rows * HD * txt,
            bytes_accessed=6 * txt * heads * HD,
            transcendentals=heads * rows * txt,
        ),
    )(core, q, text, values, mask)


def merge_kernel(heads, p0, p1, p2, p3, pt, lent_in, out_ref, lent_ref):
    parts = (p0, p1, p2, p3, pt)
    rows = lent_in.shape[0]
    stats = [p[rows : rows + 16].astype(jnp.float32) for p in parts]
    for head in range(heads):
        cols = head_cols(head)
        logs = [read_stat(s, head) for s in stats]
        top = functools.reduce(jnp.maximum, logs)
        weights = [jnp.exp2(log - top) for log in logs]
        inverse = 1.0 / sum(weights)
        weights = [jnp.broadcast_to(w * inverse, (HD, rows)).T for w in weights]
        result = 0.0
        for p, w in zip(parts, weights):
            result = result + p[0:rows, cols].astype(jnp.float32) * w
        out_ref[:, cols] = result
        lent_ref[:, cols] = (lent_in[:, cols].astype(jnp.float32) * weights[-1]).astype(jnp.bfloat16)


def merge(parts, lent, heads):
    rows = lent.shape[0]
    return pl.pallas_call(
        functools.partial(merge_kernel, heads),
        out_shape=(
            jax.ShapeDtypeStruct((rows, heads * HD), jnp.float32),
            jax.ShapeDtypeStruct((rows, heads * HD), jnp.bfloat16),
        ),
        in_specs=[VM] * 6,
        out_specs=(VM, VM),
        compiler_params=params(),
    )(*parts, lent)


def ring(n, step):
    return [(i, (i + step) % n) for i in range(n)]


def gather_ring(x, axis, n):
    near = {s: lax.ppermute(x, axis, ring(n, s)) for s in (1, n - 1)}
    half = x.shape[0] // 2
    far = [
        lax.ppermute(near[1][:half], axis, ring(n, 1)),
        lax.ppermute(near[n - 1][half:], axis, ring(n, n - 1)),
    ]
    return {1: [near[1]], n // 2: far, n - 1: [near[n - 1]]}


def body(q_img, k_img, v_img, k_txt, v_txt, replace_cols, shared_flags):
    groups = lax.axis_size("z_lo") * lax.axis_size("x")
    n_y, n_z = lax.axis_size("y"), lax.axis_size("z_hi")
    heads = H // groups
    width = heads * HD
    axes = ("z_lo", "x", "core")
    own_text = jnp.concatenate([k_txt, v_txt], axis=0)
    other_text = lax.ppermute(own_text, "core", [(0, 1), (1, 0)])
    packed = pack(q_img, k_img, v_img, groups)
    held = lax.all_to_all(packed, axes, split_axis=0, concat_axis=0, tiled=True)
    rows = held.shape[0] * held.shape[1]
    place = jnp.stack([lax.axis_index(a) for a in ("z_hi", "core")]).astype(jnp.int32)
    q, k, v = split(place[1:], held.reshape(rows, 3 * width), own_text, other_text)
    qs = {0: [q]} | gather_ring(q, "z_hi", n_z)
    up, down = ring(n_y, 1), ring(n_y, n_y - 1)
    keys = [k, lax.ppermute(k, "y", up), lax.ppermute(k, "y", down)]
    values = [v, lax.ppermute(v, "y", up), lax.ppermute(v, "y", down)]
    keys.append(lax.ppermute(keys[1], "y", up))
    values.append(lax.ppermute(values[2], "y", down))
    flags = shared_flags.reshape(1, -1)
    mask_from = (place[:1], replace_cols, flags)
    *near, mask = block_attention([qs[1], qs[3]], keys, values, rows, heads, [], mask_from=mask_from)
    far, own, text = block_attention([qs[2], qs[0]], keys, values, rows, heads, near, [qs[i] for i in range(n_z)])
    parts = [lax.ppermute(x, "z_hi", ring(n_z, n_z - s)) for s, x in ((1, near[0]), (3, near[1]), (2, far))]
    text = lax.all_gather(text, "y")
    values = lax.all_gather(text[:, 1], "core")
    txt_part, lent = text_attention(place[1:], q, text, values, mask, rows, heads)
    result, lent = merge([own] + parts + [txt_part], lent, heads)
    borrowed = lax.ppermute(lent, "core", [(0, 1)])
    result = (result + borrowed.astype(jnp.float32)).astype(jnp.bfloat16)
    result = result.reshape(2 * groups, rows // (2 * groups), width)
    back = lax.all_to_all(result, axes, split_axis=0, concat_axis=0, tiled=True)
    return unpack(back, groups)


def solution(mesh):
    fine = Mesh(mesh.devices.reshape(4, 4, 2, 2, 4), ("y", "z_hi", "core", "z_lo", "x"))
    seq, head = ("y", "z_hi", "core"), ("z_lo", "x")
    tokens = P(None, seq + head, None)
    text = P(None, seq, head)
    return jax.shard_map(
        body,
        mesh=fine,
        in_specs=(tokens, tokens, tokens, text, text, P(), P()),
        out_specs=tokens,
        check_vma=False,
    )
```
